32 devices in a mesh: groups: 2 (over y), pts: 4 (over z), cent: 4 (over x, core).
Axes of the slice: x: 2, y: 2, z: 4, core: 2. Of those that a mesh axis runs over, the one named last changes fastest.
Arguments:
- point_codes: bfloat16 [4096, 1024], P(('groups', 'pts')), parts along dimension 0, may hold values from -6 to 6
- shard_scales: float32 [16], P(('groups', 'pts')), parts along dimension 0, may hold values from 0.3 to 10
- coarse_centroids: bfloat16 [512, 1024], P('groups'), parts along dimension 0, may hold values from -1.5 to 1.5
- fine_centroids: bfloat16 [2048, 1024], P(('groups', 'pts'), 'cent'), parts along dimension 0, may hold values from -1.5 to 1.5
- block_lists: int32 [8, 16], P(('groups', 'pts')), parts along dimension 0, may hold values from 0 to 15, as said below
- live_counts: int32 [8], P(('groups', 'pts')), parts along dimension 0, may hold values from 1 to 16, as said below
Outputs:
- new_coarse: float32 [512, 1024], P(('groups', 'cent')), parts along dimension 0
- new_fine: float32 [2048, 1024], P(('groups', 'pts'), 'cent'), parts along dimension 0
The draws below stay inside these ranges and needn't reach their ends.
There are 2 independent parts, one for each index of `groups`. The reference program is written for one: setup_inputs(seed, part) draws one part's arguments, and reference() takes and returns one part's arrays. A program takes and returns all parts, laid end to end along the dimension named above; each array names one. Nothing has to cross between parts.
Inputs may be any that keep to these rules, and one draw needn't show every extreme that they name: `block_lists`: within a row the entries are distinct, and at most 4 of them lie in any range q * 4 to q * 4 + 3; some such range holds 4 entries of every row, among them the first entry. Entries past the live count are valid block numbers too. Only the first live_counts[p] entries of row p of block_lists are used.
All inputs are finite; a program needn't handle non-finite values.
Results may differ from the reference program's by a relative error of at most 0.0028.
Values may be sent and summed in bfloat16 or wider, within the bound.
A program may use at most 64 MiB of HBM per device.

```python
import jax
import jax.numpy as jnp
from jax import lax

D = 1024
NCOARSE = 256
BLOCK = 64
BLK_OWN = 4
SHARD = 256
PTS_DEV = 512
NPTS = 2048
NSHARD = 8
FINE = 1024
CAP = 16
N_PTS = 4


def draw_shard_scales(key, part):
    key = jax.random.fold_in(key, 11)
    lowest, highest = (0.5, 5.0)
    unit_draw = jax.random.uniform(key, (NSHARD,), jnp.float32)
    return jnp.exp(jnp.log(lowest) + unit_draw * (jnp.log(highest) - jnp.log(lowest))).astype(jnp.float32)


def one_order(row_key):
    return jax.random.permutation(row_key, N_PTS)


def draw_block_lists(key, part):
    key = jax.random.fold_in(key, 12)
    key_lead, key_perm, key_shift = jax.random.split(key, 3)
    leader = jax.random.randint(key_lead, (), 0, N_PTS)
    row_keys = jax.random.split(key_perm, N_PTS)
    orders = jax.vmap(one_order)(row_keys).astype(jnp.int32)
    lead_place = jnp.argmax(orders == leader, axis=1)
    first_owner = orders[:, 0]
    columns = jnp.arange(N_PTS)[None, :]
    orders = jnp.where(columns == lead_place[:, None], first_owner[:, None], orders)
    orders = orders.at[:, 0].set(leader)
    shifts = jax.random.randint(key_shift, (N_PTS, N_PTS), 0, BLK_OWN)
    slot_ids = jnp.arange(CAP)
    owner_ids = orders[:, slot_ids % N_PTS]
    local_index = (jnp.take_along_axis(shifts, owner_ids, axis=1) + slot_ids[None, :] // N_PTS) % BLK_OWN
    return (owner_ids * BLK_OWN + local_index).astype(jnp.int32)


def draw_live_counts(key, part):
    key = jax.random.fold_in(key, 13)
    key_count, key_full = jax.random.split(key)
    drawn = jax.random.randint(key_count, (N_PTS,), 1, CAP + 1)
    full_row = jax.random.randint(key_full, (), 0, N_PTS)
    return drawn.at[full_row].set(CAP).astype(jnp.int32)


def block_levels(key, dims, cuts, least, top_value):
    def one(position, shards_of):
        steps = jax.random.uniform(jax.random.fold_in(jax.random.fold_in(key, 6), position), (shards_of,), jnp.float32, least / len(cuts), top_value / len(cuts))
        return jnp.repeat(jnp.exp(steps), dims[position] // shards_of).reshape((-1,) + (1,) * (len(dims) - position - 1))

    loudness = one(*cuts[0])
    for cut in cuts[1:]:
        loudness = loudness * one(*cut)
    return loudness


def noise(stream_key, shape, width, reach, pieces=(), held_as=jnp.bfloat16):
    factor_of = block_levels(stream_key, shape, pieces, -0.22, 0.18) if pieces else 1.0
    entries = jax.random.normal(stream_key, shape, jnp.float32) * width * factor_of
    return jnp.minimum(jnp.maximum(entries, -reach), reach).astype(held_as)


def setup_inputs(seed: int = 0, part: int = 0) -> dict:
    keys = jax.random.split(jax.random.key(seed), 7)
    own_keys = jax.random.split(jax.random.fold_in(keys[6], part), 7)
    return {
        "point_codes": noise(own_keys[0], (NPTS, D), 1.0, 6.0, ((0, 4),)),
        "shard_scales": draw_shard_scales(jax.random.fold_in(jax.random.fold_in(keys[6], part), 71), part),
        "coarse_centroids": noise(own_keys[2], (NCOARSE, D), 0.25, 1.5),
        "fine_centroids": noise(own_keys[3], (FINE, D), 0.25, 1.5, ((0, 4), (1, 4))),
        "block_lists": draw_block_lists(jax.random.fold_in(jax.random.fold_in(keys[6], part), 71), part),
        "live_counts": draw_live_counts(jax.random.fold_in(jax.random.fold_in(keys[6], part), 71), part),
    }


PRIOR_MASS = 1.0
MASK_SCORE = -1.0e30


def reference(point_codes, shard_scales, coarse_centroids, fine_centroids, block_lists, live_counts):
    capacity = block_lists.shape[1]
    block_total = FINE // BLOCK
    per_tile = PTS_DEV // SHARD
    coarse_float = coarse_centroids.astype(jnp.float32)
    coarse_half = 0.5 * jnp.sum(coarse_float * coarse_float, axis=1)
    fine_blocks = fine_centroids.reshape(block_total, BLOCK, D)
    fine_half = 0.5 * jnp.sum(jnp.square(fine_blocks.astype(jnp.float32)), axis=2)
    slot_index = jnp.arange(capacity, dtype=jnp.int32)

    def tile_step(carry, inputs):
        coarse_sum, coarse_mass, fine_sum, fine_mass = carry
        tile_index, tile_list, tile_count = inputs
        tile_codes = lax.dynamic_slice_in_dim(point_codes, (tile_index * PTS_DEV).astype(jnp.int32), PTS_DEV, 0)
        tile_scales = lax.dynamic_slice_in_dim(shard_scales, (tile_index * per_tile).astype(jnp.int32), per_tile, 0)
        row_scale = jnp.repeat(tile_scales, SHARD)
        coarse_score = row_scale[:, None] * jnp.dot(tile_codes, coarse_centroids.T, preferred_element_type=jnp.float32) - coarse_half[None, :]
        coarse_peak = jnp.max(coarse_score, axis=1, keepdims=True)
        coarse_exp = jnp.exp(coarse_score - coarse_peak)
        coarse_resp = coarse_exp / jnp.sum(coarse_exp, axis=1, keepdims=True)
        coarse_weight = (coarse_resp * row_scale[:, None]).astype(jnp.bfloat16)
        coarse_sum = coarse_sum + jnp.dot(coarse_weight.T, tile_codes, preferred_element_type=jnp.float32)
        coarse_mass = coarse_mass + jnp.sum(coarse_resp, axis=0)
        chosen_blocks = fine_blocks[tile_list]
        fine_score = row_scale[:, None] * jnp.dot(tile_codes, chosen_blocks.reshape(capacity * BLOCK, D).T, preferred_element_type=jnp.float32)
        fine_score = fine_score.reshape(PTS_DEV, capacity, BLOCK) - fine_half[tile_list][None]
        block_peak = jnp.max(fine_score, axis=2, keepdims=True)
        block_norm = block_peak + jnp.log(jnp.sum(jnp.exp(fine_score - block_peak), axis=2, keepdims=True))
        parent_score = coarse_score[:, tile_list % NCOARSE]
        joint_score = parent_score[:, :, None] + fine_score - block_norm
        live_slot = slot_index < tile_count
        joint_score = jnp.where(live_slot[None, :, None], joint_score, MASK_SCORE).reshape(PTS_DEV, capacity * BLOCK)
        joint_peak = jnp.max(joint_score, axis=1, keepdims=True)
        joint_exp = jnp.exp(joint_score - joint_peak)
        fine_resp = joint_exp / jnp.sum(joint_exp, axis=1, keepdims=True)
        fine_weight = (fine_resp * row_scale[:, None]).astype(jnp.bfloat16)
        tile_sums = jnp.dot(fine_weight.T, tile_codes, preferred_element_type=jnp.float32).reshape(capacity, BLOCK, D)
        fine_sum = fine_sum.at[tile_list].add(tile_sums)
        fine_mass = fine_mass.at[tile_list].add(jnp.sum(fine_resp, axis=0).reshape(capacity, BLOCK))
        return (coarse_sum, coarse_mass, fine_sum, fine_mass), None

    start_carry = (jnp.zeros((NCOARSE, D), jnp.float32), jnp.zeros((NCOARSE,), jnp.float32),
                   jnp.zeros((block_total, BLOCK, D), jnp.float32), jnp.zeros((block_total, BLOCK), jnp.float32))
    tile_ids = jnp.arange(N_PTS, dtype=jnp.int32)
    final_carry, unused_out = lax.scan(tile_step, start_carry, (tile_ids, block_lists, live_counts))
    coarse_sum, coarse_mass, fine_sum, fine_mass = final_carry
    new_coarse = (coarse_sum + PRIOR_MASS * coarse_float) / (coarse_mass[:, None] + PRIOR_MASS)
    fine_float = fine_blocks.astype(jnp.float32)
    new_fine = (fine_sum + PRIOR_MASS * fine_float) / (fine_mass[:, :, None] + PRIOR_MASS)
    return (new_coarse, new_fine.reshape(FINE, D))
```

```python
import functools

import jax
import jax.numpy as jnp
from jax import lax
from jax.experimental import pallas as pl
from jax.experimental.pallas import tpu as pltpu
from jax.sharding import PartitionSpec as P

NCOARSE = 256
BLOCK = 64
SHARD = 256


PRIOR_MASS = 1.0
MASK_SCORE = -1e30


def joined(part, axis, combine):
    gathered = jax.tree.map(lambda a: lax.all_gather(a, axis), part)

    def take(source):
        return jax.tree.map(lambda a: lax.dynamic_index_in_dim(a, source, 0, False), gathered)

    return lax.fori_loop(
        1, lax.axis_size(axis), lambda source, state: combine(state, take(source)), take(0)
    )


def combine_norms(first_part, second_part):
    peak_value = jnp.maximum(first_part[0], second_part[0])
    scaled = first_part[1] * jnp.exp(first_part[0] - peak_value) + second_part[1] * jnp.exp(
        second_part[0] - peak_value
    )
    return (peak_value, scaled)


def rank_within(owner_ids):
    width_n = owner_ids.shape[-1]
    earlier_mask = jnp.arange(width_n)[None, :] < jnp.arange(width_n)[:, None]
    same_owner = owner_ids[..., :, None] == owner_ids[..., None, :]
    return jnp.sum(jnp.logical_and(same_owner, earlier_mask), axis=-1)


def owner_selection(owner_ids, local_index, chosen, pair_slots, own_blocks):
    rank_values = rank_within(owner_ids)
    by_rank = jnp.logical_and(
        chosen[..., None], rank_values[..., None] == jnp.arange(pair_slots)
    ).astype(jnp.float32)
    by_block = (local_index[..., None] == jnp.arange(own_blocks)).astype(jnp.float32)
    return jnp.einsum("psr,psl->prl", by_rank, by_block).reshape(-1, own_blocks)


def general_body(point_codes, shard_scales, coarse_centroids, fine_centroids, block_lists, live_counts):
    pts_count = lax.axis_size("pts")
    cent_count = lax.axis_size("cent")
    pts_index = lax.axis_index("pts")
    cent_index = lax.axis_index("cent")
    point_count, width_d = point_codes.shape
    own_blocks = fine_centroids.shape[0] // BLOCK
    quarter = fine_centroids.shape[1]
    capacity = block_lists.shape[1]
    my_slots = capacity // cent_count
    pair_slots = max(1, capacity // pts_count)
    row_scale = jnp.repeat(shard_scales, SHARD)
    all_lists = lax.all_gather(block_lists, "pts", axis=0, tiled=True)
    coarse_share = NCOARSE // cent_count
    coarse_mine = lax.dynamic_slice_in_dim(
        coarse_centroids, cent_index * coarse_share, coarse_share, 0
    )
    half_mine = 0.5 * jnp.sum(jnp.square(coarse_mine.astype(jnp.float32)), axis=1)
    coarse_score = (
        row_scale[:, None]
        * jnp.einsum("pd,kd->pk", point_codes, coarse_mine, preferred_element_type=jnp.float32)
        - half_mine[None, :]
    )
    local_peak = jnp.max(coarse_score, axis=1)
    local_total = jnp.sum(jnp.exp(coarse_score - local_peak[:, None]), axis=1)
    coarse_peak, coarse_total = joined((local_peak, local_total), "cent", combine_norms)
    coarse_resp = jnp.exp(coarse_score - coarse_peak[:, None]) / coarse_total[:, None]
    coarse_weight = (coarse_resp * row_scale[:, None]).astype(jnp.bfloat16)
    coarse_sum = jnp.einsum(
        "pk,pd->kd", coarse_weight, point_codes, preferred_element_type=jnp.float32
    )
    coarse_mass = jnp.sum(coarse_resp, axis=0)
    coarse_sum, coarse_mass = lax.psum((coarse_sum, coarse_mass), "pts")
    new_coarse = (coarse_sum + PRIOR_MASS * coarse_mine.astype(jnp.float32)) / (
        coarse_mass[:, None] + PRIOR_MASS
    )
    row_list = block_lists[0]
    row_owner = row_list // own_blocks
    row_position = row_owner * pair_slots + rank_within(row_owner)
    list_owner = all_lists // own_blocks
    list_local = all_lists % own_blocks
    return_picks = owner_selection(
        list_owner, list_local, list_owner == pts_index, pair_slots, own_blocks
    )
    my_start = cent_index * my_slots
    my_blocks = lax.dynamic_slice_in_dim(row_list, my_start, my_slots, 0)
    whole_rows = lax.all_gather(fine_centroids, "cent", axis=1, tiled=True)
    in_range = jnp.arange(capacity) // my_slots == cent_index
    owner_masked = jnp.where(in_range[None, :], list_owner, -1)
    selection = owner_selection(
        owner_masked, list_local, owner_masked == pts_index, pair_slots, own_blocks
    )
    outgoing = jnp.dot(
        selection.astype(jnp.bfloat16),
        whole_rows.reshape(own_blocks, BLOCK * width_d),
        preferred_element_type=jnp.bfloat16,
    )
    arrived = lax.all_to_all(
        outgoing.reshape(pts_count * pair_slots, BLOCK, width_d),
        "pts",
        split_axis=0,
        concat_axis=0,
        tiled=True,
    )
    my_owner = my_blocks // own_blocks
    my_position = my_owner * pair_slots + rank_within(my_owner)
    block_rows = jnp.take(arrived, my_position, axis=0)
    block_flat = block_rows.reshape(my_slots * BLOCK, width_d)
    half_fine = 0.5 * jnp.sum(jnp.square(block_flat.astype(jnp.float32)), axis=1).reshape(
        my_slots, BLOCK
    )
    fine_score = row_scale[:, None] * jnp.einsum(
        "pd,jd->pj", point_codes, block_flat, preferred_element_type=jnp.float32
    )
    fine_score = fine_score.reshape(point_count, my_slots, BLOCK) - half_fine[None]
    block_peak = jnp.max(fine_score, axis=2, keepdims=True)
    block_norm = block_peak + jnp.log(
        jnp.sum(jnp.exp(fine_score - block_peak), axis=2, keepdims=True)
    )
    parent_rows = jnp.take(coarse_centroids, my_blocks % NCOARSE, axis=0)
    parent_half = 0.5 * jnp.sum(jnp.square(parent_rows.astype(jnp.float32)), axis=1)
    parent_score = (
        row_scale[:, None]
        * jnp.einsum("pd,sd->ps", point_codes, parent_rows, preferred_element_type=jnp.float32)
        - parent_half[None, :]
    )
    joint_score = parent_score[:, :, None] + fine_score - block_norm
    live_slot = my_start + jnp.arange(my_slots) < live_counts[0]
    joint_score = jnp.where(live_slot[None, :, None], joint_score, MASK_SCORE).reshape(
        point_count, my_slots * BLOCK
    )
    joint_peak = jnp.max(joint_score, axis=1)
    joint_total = jnp.sum(jnp.exp(joint_score - joint_peak[:, None]), axis=1)
    fine_peak, fine_total = joined((joint_peak, joint_total), "cent", combine_norms)
    fine_resp = jnp.exp(joint_score - fine_peak[:, None]) / fine_total[:, None]
    fine_weight = (fine_resp * row_scale[:, None]).astype(jnp.bfloat16)
    fine_sum = jnp.einsum(
        "pj,pd->jd", fine_weight, point_codes, preferred_element_type=jnp.float32
    ).reshape(my_slots, BLOCK, width_d)
    fine_mass = jnp.sum(fine_resp, axis=0).reshape(my_slots, BLOCK)
    mass_copies = jnp.broadcast_to(fine_mass[:, :, None], (my_slots, BLOCK, cent_count))
    sum_quarters, mass_quarters = (
        lax.all_to_all(fine_sum, "cent", split_axis=2, concat_axis=0, tiled=True),
        lax.all_to_all(mass_copies, "cent", split_axis=2, concat_axis=0, tiled=True),
    )
    targets = jnp.arange(pts_count * pair_slots)
    matches = row_position[None, :] == targets[:, None]
    source = jnp.sum(jnp.where(matches, jnp.arange(capacity)[None, :], 0), axis=1)
    present = jnp.any(matches, axis=1)[:, None, None]
    send_sums = jnp.where(present, jnp.take(sum_quarters, source, axis=0), 0.0)
    send_mass = jnp.where(present, jnp.take(mass_quarters, source, axis=0), 0.0)
    back_sums, back_mass = (
        lax.all_to_all(send_sums, "pts", split_axis=0, concat_axis=0, tiled=True),
        lax.all_to_all(send_mass, "pts", split_axis=0, concat_axis=0, tiled=True),
    )
    owner_sums = jnp.einsum("xl,xbq->lbq", return_picks, back_sums, precision=lax.Precision.HIGHEST)
    owner_mass = jnp.einsum("xl,xbq->lbq", return_picks, back_mass, precision=lax.Precision.HIGHEST)
    prior_rows = fine_centroids.astype(jnp.float32).reshape(own_blocks, BLOCK, quarter)
    new_fine = (owner_sums + PRIOR_MASS * prior_rows) / (owner_mass + PRIOR_MASS)
    return (new_coarse, new_fine.reshape(own_blocks * BLOCK, quarter))


def row_dot(a, b):
    return lax.dot_general(a, b, (((1,), (1,)), ((), ())), preferred_element_type=jnp.float32)


def half_square(a):
    a = a.astype(jnp.float32)
    return 0.5 * jnp.sum(a * a, axis=1, keepdims=True)


def diagonal(rows):
    shape = (rows, 128)
    return lax.broadcasted_iota(jnp.int32, shape, 0) == lax.broadcasted_iota(jnp.int32, shape, 1)


def to_row(column):
    row = jnp.sum(jnp.where(diagonal(column.shape[0]), column, 0.0), axis=0, keepdims=True)
    return jnp.broadcast_to(row, (8, 128))


def to_column(row, rows):
    return jnp.sum(jnp.where(diagonal(rows), row, 0.0), axis=1, keepdims=True)


def kernel(
    n, m,
    codes, scales, coarse, fine, lists, counts,
    out_coarse, out_fine,
    rows, sums, part, outgoing, from_left, from_right, prior, resp,
    coarse_mass, mass_out, mass_in, finished, arrived,
    x_send, x_recv, gr_send, gl_send, g_recv, cr_send, cl_send, c_recv,
    s_send, sl_recv, sr_recv, m_send, m_recv, cm_send, cm_recv, o_send, o_recv,
):
    z = lax.axis_index("pts")
    c = lax.axis_index("cent")
    right, left = lax.rem(z + 1, n), lax.rem(z + n - 1, n)
    points, width = codes.shape
    quarter = fine.shape[1]
    share = coarse.shape[0] // m

    def remote(src, dst, send, recv, target):
        return pltpu.make_async_remote_copy(
            src_ref=src, dst_ref=dst, send_sem=send, recv_sem=recv,
            device_id=target, device_id_type=pl.DeviceIdType.MESH,
        )

    def cent_peer(j):
        return lax.rem(c + j, m)

    def pts_peer(j):
        return lax.rem(z + j, n)

    def lanes(i):
        return pl.ds(pl.multiple_of(i * quarter, quarter), quarter)

    def block_rows(i):
        return pl.ds(pl.multiple_of(i * BLOCK, BLOCK), BLOCK)

    barrier = pltpu.get_barrier_semaphore()
    for j in range(1, m):
        pl.semaphore_signal(
            barrier, inc=1, device_id={"cent": cent_peer(j)}, device_id_type=pl.DeviceIdType.MESH
        )
    for j in range(1, n):
        pl.semaphore_signal(
            barrier, inc=1, device_id={"pts": pts_peer(j)}, device_id_type=pl.DeviceIdType.MESH
        )
    pl.semaphore_wait(barrier, n + m - 2)

    def features_to(peer):
        return remote(
            fine.at[block_rows(peer), :], rows.at[z, :, lanes(c)],
            x_send.at[peer], x_recv.at[c], {"cent": peer},
        )

    def features_from(peer):
        return remote(
            fine.at[block_rows(peer), :], rows.at[z, :, lanes(peer)],
            x_send.at[peer], x_recv.at[peer], {"cent": peer},
        )

    for j in range(1, m):
        features_to(cent_peer(j)).start()
    rows[z, :, lanes(c)] = fine[block_rows(c), :]

    scale_row = jnp.zeros((1, points), jnp.float32)
    shard = lax.broadcasted_iota(jnp.int32, (1, points), 1) // SHARD
    for i in range(scales.shape[1]):
        scale_row = jnp.where(shard == i, scales[0:1, i : i + 1], scale_row)

    score = scale_row * row_dot(coarse[...], codes[...]) - half_square(coarse[...])
    expo = jnp.exp(score - jnp.max(score, axis=0, keepdims=True))
    resp[...] = expo / jnp.sum(expo, axis=0, keepdims=True)
    slots = lists.shape[1]
    shape = (slots, slots)
    slot = lax.broadcasted_iota(jnp.int32, shape, 1)
    named = jnp.logical_and(
        lists[...] == lax.broadcasted_iota(jnp.int32, shape, 0), slot < counts[...]
    )
    live = jnp.sum(jnp.where(named, 1.0, 0.0), axis=1, keepdims=True) > 0.0
    parent = jnp.where(live, score[:slots], MASK_SCORE)
    parent = jnp.exp(parent - jnp.max(parent, axis=0, keepdims=True))
    parent = jnp.where(live, parent, 0.0)
    prior[...] = parent / jnp.sum(parent, axis=0, keepdims=True)

    def to_right(buffer, b, send, recv):
        return remote(buffer.at[b], buffer.at[b], send.at[b], recv.at[b], {"pts": right})

    def to_left(buffer, b, send, recv):
        return remote(buffer.at[b], buffer.at[b], send.at[b], recv.at[b], {"pts": left})

    def start_own(buffer, send_r, send_l, recv):
        @pl.when(z < n - 1)
        def _():
            to_right(buffer, z, send_r, recv).start()

        @pl.when(z > 0)
        def _():
            to_left(buffer, z, send_l, recv).start()

    def pass_on(d, buffer, send_r, send_l, recv):
        @pl.when(z - d >= 0)
        def _():
            to_right(buffer, z - d, send_r, recv).wait_recv()

            @pl.when(z < n - 1)
            def _():
                to_right(buffer, z - d, send_r, recv).start()

        @pl.when(z + d < n)
        def _():
            to_left(buffer, z + d, send_l, recv).wait_recv()

            @pl.when(z > 0)
            def _():
                to_left(buffer, z + d, send_l, recv).start()

    def finish_sends(buffer, send_r, send_l, recv):
        for d in range(n):
            @pl.when(jnp.logical_and(z - d >= 0, z < n - 1))
            def _():
                to_right(buffer, z - d, send_r, recv).wait_send()

            @pl.when(jnp.logical_and(z + d < n, z > 0))
            def _():
                to_left(buffer, z + d, send_l, recv).wait_send()

    fine_sems = (gr_send, gl_send, g_recv)
    coarse_sems = (cr_send, cl_send, c_recv)

    for j in range(1, m):
        features_from(cent_peer(j)).wait_recv()
    start_own(rows, *fine_sems)

    mine = resp[pl.ds(pl.multiple_of(c * share, share), share), :]
    sums[z] = jnp.dot(
        (mine * scale_row).astype(jnp.bfloat16), codes[...], preferred_element_type=jnp.float32
    ).astype(jnp.bfloat16)
    coarse_mass[z] = to_row(jnp.sum(mine, axis=1, keepdims=True))
    start_own(sums, *coarse_sems)

    def coarse_mass_to(peer):
        return remote(
            coarse_mass.at[z], coarse_mass.at[z], cm_send.at[peer], cm_recv.at[z], {"pts": peer}
        )

    def coarse_mass_from(peer):
        return remote(
            coarse_mass.at[peer], coarse_mass.at[peer], cm_send.at[peer], cm_recv.at[peer],
            {"pts": peer},
        )

    for j in range(1, n):
        coarse_mass_to(pts_peer(j)).start()

    def mass_to(peer):
        return remote(
            mass_out.at[peer], mass_in.at[z], m_send.at[peer], m_recv.at[z], {"pts": peer}
        )

    def mass_from(peer):
        return remote(
            mass_out.at[peer], mass_in.at[peer], m_send.at[peer], m_recv.at[peer], {"pts": peer}
        )

    def use_block(b):
        block = rows[b]
        score = scale_row * row_dot(block, codes[...]) - half_square(block)
        expo = jnp.exp(score - jnp.max(score, axis=0, keepdims=True))
        factor = prior[pl.ds(b * m + c, 1), :] / jnp.sum(expo, axis=0, keepdims=True)
        share_of = expo * factor
        part[b] = jnp.dot(
            (share_of * scale_row).astype(jnp.bfloat16), codes[...],
            preferred_element_type=jnp.float32,
        )
        return to_row(jnp.sum(share_of, axis=1, keepdims=True))

    def sums_right(b):
        return remote(
            outgoing.at[b], from_left.at[b], s_send.at[b], sl_recv.at[b], {"pts": right}
        )

    def sums_left(b):
        return remote(
            outgoing.at[b], from_right.at[b], s_send.at[b], sr_recv.at[b], {"pts": left}
        )

    mass_in[z] = use_block(z)
    for d in range(1, n):
        pass_on(d, rows, *fine_sems)

        @pl.when(z - d >= 0)
        def _():
            b = z - d
            mass_out[b] = use_block(b)
            mass_to(b).start()

            @pl.when(z == n - 1)
            def _():
                outgoing[b] = part[b].astype(jnp.bfloat16)
                sums_left(b).start()

        @pl.when(z + d < n)
        def _():
            b = z + d
            mass_out[b] = use_block(b)
            mass_to(b).start()

            @pl.when(z == 0)
            def _():
                outgoing[b] = part[b].astype(jnp.bfloat16)
                sums_right(b).start()

        pass_on(d, sums, *coarse_sems)

    mirror = n - 1 - z
    for time in range(3, 2 * n - 2):
        @pl.when(jnp.logical_and(z > 0, jnp.logical_and(time - z > z, time - z < n)))
        def _():
            b = time - z
            sums_right(b).wait_recv()
            outgoing[b] = (part[b] + from_left[b].astype(jnp.float32)).astype(jnp.bfloat16)
            sums_right(b).start()

        @pl.when(
            jnp.logical_and(mirror > 0, jnp.logical_and(time - mirror > mirror, time - mirror < n))
        )
        def _():
            b = n - 1 - (time - mirror)
            sums_left(b).wait_recv()
            outgoing[b] = (part[b] + from_right[b].astype(jnp.float32)).astype(jnp.bfloat16)
            sums_left(b).start()

    for j in range(1, n):
        coarse_mass_from(pts_peer(j)).wait_recv()
    total = sums[0].astype(jnp.float32)
    mass = coarse_mass[0]
    for i in range(1, n):
        total = total + sums[i].astype(jnp.float32)
        mass = mass + coarse_mass[i]
    own = coarse[pl.ds(pl.multiple_of(c * share, share), share), :].astype(jnp.float32)
    out_coarse[...] = (total + PRIOR_MASS * own) / (to_column(mass[0:1], share) + PRIOR_MASS)

    for j in range(1, n):
        mass_from(pts_peer(j)).wait_recv()

    @pl.when(z > 0)
    def _():
        sums_right(z).wait_recv()
        part[z] = part[z] + from_left[z].astype(jnp.float32)

    @pl.when(z < n - 1)
    def _():
        sums_left(z).wait_recv()
        part[z] = part[z] + from_right[z].astype(jnp.float32)

    mass = mass_in[0]
    for i in range(1, n):
        mass = mass + mass_in[i]
    finished[...] = (part[z] + PRIOR_MASS * rows[z].astype(jnp.float32)) / (
        to_column(mass[0:1], BLOCK) + PRIOR_MASS
    )

    def result_to(peer):
        return remote(
            finished.at[:, lanes(peer)], arrived.at[c], o_send.at[peer], o_recv.at[c],
            {"cent": peer},
        )

    def result_from(peer):
        return remote(
            finished.at[:, lanes(peer)], arrived.at[peer], o_send.at[peer], o_recv.at[peer],
            {"cent": peer},
        )

    for j in range(1, m):
        result_to(cent_peer(j)).start()
    out_fine[block_rows(c), :] = finished[:, lanes(c)]

    for j in range(1, m):
        features_to(cent_peer(j)).wait_send()
    finish_sends(rows, *fine_sems)
    finish_sends(sums, *coarse_sems)
    for j in range(1, n):
        coarse_mass_to(pts_peer(j)).wait_send()
        mass_to(pts_peer(j)).wait_send()
    for d in range(1, n):
        @pl.when(z + d < n)
        def _():
            sums_right(z + d).wait_send()

        @pl.when(z - d >= 0)
        def _():
            sums_left(z - d).wait_send()

    for j in range(1, m):
        peer = cent_peer(j)
        result_from(peer).wait_recv()
        out_fine[block_rows(peer), :] = arrived[peer]
    for j in range(1, m):
        result_to(cent_peer(j)).wait_send()


def body(point_codes, shard_scales, coarse_centroids, fine_centroids, block_lists, live_counts):
    n = lax.axis_size("pts")
    m = lax.axis_size("cent")
    points, width = point_codes.shape
    own_blocks = fine_centroids.shape[0] // BLOCK
    quarter = fine_centroids.shape[1]
    slots = block_lists.shape[1]
    every_block = slots == n * own_blocks and own_blocks == m and slots <= NCOARSE
    if not every_block:
        return general_body(
            point_codes, shard_scales, coarse_centroids, fine_centroids, block_lists, live_counts
        )
    share = NCOARSE // m
    f32, bf16 = jnp.float32, jnp.bfloat16
    dma = pltpu.SemaphoreType.DMA
    vmem = pl.BlockSpec(memory_space=pltpu.VMEM)
    return pl.pallas_call(
        functools.partial(kernel, n, m),
        out_shape=(
            jax.ShapeDtypeStruct((share, width), f32),
            jax.ShapeDtypeStruct((own_blocks * BLOCK, quarter), f32),
        ),
        in_specs=[vmem] * 6,
        out_specs=(vmem, vmem),
        scratch_shapes=[
            pltpu.VMEM((n, BLOCK, width), bf16),
            pltpu.VMEM((n, share, width), bf16),
            pltpu.VMEM((n, BLOCK, width), f32),
            pltpu.VMEM((n, BLOCK, width), bf16),
            pltpu.VMEM((n, BLOCK, width), bf16),
            pltpu.VMEM((n, BLOCK, width), bf16),
            pltpu.VMEM((slots, points), f32),
            pltpu.VMEM((NCOARSE, points), f32),
            pltpu.VMEM((n, 8, 128), f32),
            pltpu.VMEM((n, 8, 128), f32),
            pltpu.VMEM((n, 8, 128), f32),
            pltpu.VMEM((BLOCK, width), f32),
            pltpu.VMEM((m, BLOCK, quarter), f32),
        ]
        + [dma((m,))] * 2
        + [dma((n,))] * 13
        + [dma((m,))] * 2,
        compiler_params=pltpu.CompilerParams(
            collective_id=0, has_side_effects=True, vmem_limit_bytes=40 * 1024 * 1024
        ),
    )(
        point_codes,
        shard_scales.reshape(1, -1),
        coarse_centroids,
        fine_centroids,
        block_lists,
        live_counts.reshape(1, 1),
    )


def solution(mesh):
    return jax.shard_map(
        body,
        mesh=mesh,
        in_specs=(
            P(("groups", "pts"), None),
            P(("groups", "pts")),
            P("groups", None),
            P(("groups", "pts"), "cent"),
            P(("groups", "pts"), None),
            P(("groups", "pts")),
        ),
        out_specs=(P(("groups", "cent"), None), P(("groups", "pts"), "cent")),
        check_vma=False,
    )
```

```python
import functools

import jax
import jax.numpy as jnp
from jax import lax
from jax.experimental import pallas as pl
from jax.experimental.pallas import tpu as pltpu
from jax.sharding import PartitionSpec as P

NCOARSE = 256
BLOCK = 64
SHARD = 256


PRIOR_MASS = 1.0
MASK_SCORE = -1e30
HALVES = 2


def joined(part, axis, combine):
    gathered = jax.tree.map(lambda a: lax.all_gather(a, axis), part)

    def take(source):
        return jax.tree.map(lambda a: lax.dynamic_index_in_dim(a, source, 0, False), gathered)

    return lax.fori_loop(
        1, lax.axis_size(axis), lambda source, state: combine(state, take(source)), take(0)
    )


def combine_norms(first_part, second_part):
    peak_value = jnp.maximum(first_part[0], second_part[0])
    scaled = first_part[1] * jnp.exp(first_part[0] - peak_value) + second_part[1] * jnp.exp(
        second_part[0] - peak_value
    )
    return (peak_value, scaled)


def rank_within(owner_ids):
    width_n = owner_ids.shape[-1]
    earlier_mask = jnp.arange(width_n)[None, :] < jnp.arange(width_n)[:, None]
    same_owner = owner_ids[..., :, None] == owner_ids[..., None, :]
    return jnp.sum(jnp.logical_and(same_owner, earlier_mask), axis=-1)


def owner_selection(owner_ids, local_index, chosen, pair_slots, own_blocks):
    rank_values = rank_within(owner_ids)
    by_rank = jnp.logical_and(
        chosen[..., None], rank_values[..., None] == jnp.arange(pair_slots)
    ).astype(jnp.float32)
    by_block = (local_index[..., None] == jnp.arange(own_blocks)).astype(jnp.float32)
    return jnp.einsum("psr,psl->prl", by_rank, by_block).reshape(-1, own_blocks)


def general_body(point_codes, shard_scales, coarse_centroids, fine_centroids, block_lists, live_counts):
    pts_count = lax.axis_size("pts")
    cent_count = lax.axis_size("cent")
    pts_index = lax.axis_index("pts")
    cent_index = lax.axis_index("cent")
    point_count, width_d = point_codes.shape
    own_blocks = fine_centroids.shape[0] // BLOCK
    quarter = fine_centroids.shape[1]
    capacity = block_lists.shape[1]
    my_slots = capacity // cent_count
    pair_slots = max(1, capacity // pts_count)
    row_scale = jnp.repeat(shard_scales, SHARD)
    all_lists = lax.all_gather(block_lists, "pts", axis=0, tiled=True)
    coarse_share = NCOARSE // cent_count
    coarse_mine = lax.dynamic_slice_in_dim(
        coarse_centroids, cent_index * coarse_share, coarse_share, 0
    )
    half_mine = 0.5 * jnp.sum(jnp.square(coarse_mine.astype(jnp.float32)), axis=1)
    coarse_score = (
        row_scale[:, None]
        * jnp.einsum("pd,kd->pk", point_codes, coarse_mine, preferred_element_type=jnp.float32)
        - half_mine[None, :]
    )
    local_peak = jnp.max(coarse_score, axis=1)
    local_total = jnp.sum(jnp.exp(coarse_score - local_peak[:, None]), axis=1)
    coarse_peak, coarse_total = joined((local_peak, local_total), "cent", combine_norms)
    coarse_resp = jnp.exp(coarse_score - coarse_peak[:, None]) / coarse_total[:, None]
    coarse_weight = (coarse_resp * row_scale[:, None]).astype(jnp.bfloat16)
    coarse_sum = jnp.einsum(
        "pk,pd->kd", coarse_weight, point_codes, preferred_element_type=jnp.float32
    )
    coarse_mass = jnp.sum(coarse_resp, axis=0)
    coarse_sum, coarse_mass = lax.psum((coarse_sum, coarse_mass), "pts")
    new_coarse = (coarse_sum + PRIOR_MASS * coarse_mine.astype(jnp.float32)) / (
        coarse_mass[:, None] + PRIOR_MASS
    )
    row_list = block_lists[0]
    row_owner = row_list // own_blocks
    row_position = row_owner * pair_slots + rank_within(row_owner)
    list_owner = all_lists // own_blocks
    list_local = all_lists % own_blocks
    return_picks = owner_selection(
        list_owner, list_local, list_owner == pts_index, pair_slots, own_blocks
    )
    my_start = cent_index * my_slots
    my_blocks = lax.dynamic_slice_in_dim(row_list, my_start, my_slots, 0)
    whole_rows = lax.all_gather(fine_centroids, "cent", axis=1, tiled=True)
    in_range = jnp.arange(capacity) // my_slots == cent_index
    owner_masked = jnp.where(in_range[None, :], list_owner, -1)
    selection = owner_selection(
        owner_masked, list_local, owner_masked == pts_index, pair_slots, own_blocks
    )
    outgoing = jnp.dot(
        selection.astype(jnp.bfloat16),
        whole_rows.reshape(own_blocks, BLOCK * width_d),
        preferred_element_type=jnp.bfloat16,
    )
    arrived = lax.all_to_all(
        outgoing.reshape(pts_count * pair_slots, BLOCK, width_d),
        "pts",
        split_axis=0,
        concat_axis=0,
        tiled=True,
    )
    my_owner = my_blocks // own_blocks
    my_position = my_owner * pair_slots + rank_within(my_owner)
    block_rows = jnp.take(arrived, my_position, axis=0)
    block_flat = block_rows.reshape(my_slots * BLOCK, width_d)
    half_fine = 0.5 * jnp.sum(jnp.square(block_flat.astype(jnp.float32)), axis=1).reshape(
        my_slots, BLOCK
    )
    fine_score = row_scale[:, None] * jnp.einsum(
        "pd,jd->pj", point_codes, block_flat, preferred_element_type=jnp.float32
    )
    fine_score = fine_score.reshape(point_count, my_slots, BLOCK) - half_fine[None]
    block_peak = jnp.max(fine_score, axis=2, keepdims=True)
    block_norm = block_peak + jnp.log(
        jnp.sum(jnp.exp(fine_score - block_peak), axis=2, keepdims=True)
    )
    parent_rows = jnp.take(coarse_centroids, my_blocks % NCOARSE, axis=0)
    parent_half = 0.5 * jnp.sum(jnp.square(parent_rows.astype(jnp.float32)), axis=1)
    parent_score = (
        row_scale[:, None]
        * jnp.einsum("pd,sd->ps", point_codes, parent_rows, preferred_element_type=jnp.float32)
        - parent_half[None, :]
    )
    joint_score = parent_score[:, :, None] + fine_score - block_norm
    live_slot = my_start + jnp.arange(my_slots) < live_counts[0]
    joint_score = jnp.where(live_slot[None, :, None], joint_score, MASK_SCORE).reshape(
        point_count, my_slots * BLOCK
    )
    joint_peak = jnp.max(joint_score, axis=1)
    joint_total = jnp.sum(jnp.exp(joint_score - joint_peak[:, None]), axis=1)
    fine_peak, fine_total = joined((joint_peak, joint_total), "cent", combine_norms)
    fine_resp = jnp.exp(joint_score - fine_peak[:, None]) / fine_total[:, None]
    fine_weight = (fine_resp * row_scale[:, None]).astype(jnp.bfloat16)
    fine_sum = jnp.einsum(
        "pj,pd->jd", fine_weight, point_codes, preferred_element_type=jnp.float32
    ).reshape(my_slots, BLOCK, width_d)
    fine_mass = jnp.sum(fine_resp, axis=0).reshape(my_slots, BLOCK)
    mass_copies = jnp.broadcast_to(fine_mass[:, :, None], (my_slots, BLOCK, cent_count))
    sum_quarters, mass_quarters = (
        lax.all_to_all(fine_sum, "cent", split_axis=2, concat_axis=0, tiled=True),
        lax.all_to_all(mass_copies, "cent", split_axis=2, concat_axis=0, tiled=True),
    )
    targets = jnp.arange(pts_count * pair_slots)
    matches = row_position[None, :] == targets[:, None]
    source = jnp.sum(jnp.where(matches, jnp.arange(capacity)[None, :], 0), axis=1)
    present = jnp.any(matches, axis=1)[:, None, None]
    send_sums = jnp.where(present, jnp.take(sum_quarters, source, axis=0), 0.0)
    send_mass = jnp.where(present, jnp.take(mass_quarters, source, axis=0), 0.0)
    back_sums, back_mass = (
        lax.all_to_all(send_sums, "pts", split_axis=0, concat_axis=0, tiled=True),
        lax.all_to_all(send_mass, "pts", split_axis=0, concat_axis=0, tiled=True),
    )
    owner_sums = jnp.einsum("xl,xbq->lbq", return_picks, back_sums, precision=lax.Precision.HIGHEST)
    owner_mass = jnp.einsum("xl,xbq->lbq", return_picks, back_mass, precision=lax.Precision.HIGHEST)
    prior_rows = fine_centroids.astype(jnp.float32).reshape(own_blocks, BLOCK, quarter)
    new_fine = (owner_sums + PRIOR_MASS * prior_rows) / (owner_mass + PRIOR_MASS)
    return (new_coarse, new_fine.reshape(own_blocks * BLOCK, quarter))


def row_dot(a, b):
    return lax.dot_general(a, b, (((1,), (1,)), ((), ())), preferred_element_type=jnp.float32)


def half_square(a):
    a = a.astype(jnp.float32)
    return 0.5 * jnp.sum(a * a, axis=1, keepdims=True)


def diagonal(rows, start=0):
    shape = (rows, 128)
    row = lax.broadcasted_iota(jnp.int32, shape, 0) + start
    return row == lax.broadcasted_iota(jnp.int32, shape, 1)


def to_row(column):
    row = jnp.sum(jnp.where(diagonal(column.shape[0]), column, 0.0), axis=0, keepdims=True)
    return jnp.broadcast_to(row, (8, 128))


def to_column(row, rows, start=0):
    return jnp.sum(jnp.where(diagonal(rows, start), row, 0.0), axis=1, keepdims=True)


def kernel(
    n, m,
    codes_in, scales, coarse_in, fine, lists, counts,
    out_coarse, out_fine,
    codes, coarse, rows, own_part, outgoing, incoming, prior, resp,
    coarse_out, coarse_own, coarse_in_sums, coarse_new,
    coarse_mass, mass_out, mass_in, finished, arrived,
    in_sem, x_send, x_recv, gr_send, gl_send, g_recv,
    cs_send, cs_recv, cg_send, cg_recv,
    s_send, s_recv, m_send, m_recv, cm_send, cm_recv, o_send, o_recv,
):
    z = lax.axis_index("pts")
    c = lax.axis_index("cent")
    right, left = lax.rem(z + 1, n), lax.rem(z + n - 1, n)
    points, width = codes.shape
    quarter = fine.shape[1]
    share = coarse.shape[0] // m
    piece = share // n
    half = BLOCK // HALVES

    def remote(src, dst, send, recv, target):
        return pltpu.make_async_remote_copy(
            src_ref=src, dst_ref=dst, send_sem=send, recv_sem=recv,
            device_id=target, device_id_type=pl.DeviceIdType.MESH,
        )

    def cent_peer(j):
        return lax.rem(c + j, m)

    def pts_peer(j):
        return lax.rem(z + j, n)

    def lanes(i):
        return pl.ds(pl.multiple_of(i * quarter, quarter), quarter)

    def block_rows(i):
        return pl.ds(pl.multiple_of(i * BLOCK, BLOCK), BLOCK)

    barrier = pltpu.get_barrier_semaphore()
    copies = [
        pltpu.make_async_copy(coarse_in, coarse, in_sem.at[0]),
        pltpu.make_async_copy(codes_in, codes, in_sem.at[1]),
        pltpu.make_async_copy(fine.at[block_rows(c), :], rows.at[z, :, lanes(c)], in_sem.at[2]),
    ]
    for j in range(1, m):
        pl.semaphore_signal(
            barrier, inc=1, device_id={"cent": cent_peer(j)}, device_id_type=pl.DeviceIdType.MESH
        )
    for j in range(1, n):
        pl.semaphore_signal(
            barrier, inc=1, device_id={"pts": pts_peer(j)}, device_id_type=pl.DeviceIdType.MESH
        )
    for copy in copies:
        copy.start()
    pl.semaphore_wait(barrier, n + m - 2)

    def features_to(peer):
        return remote(
            fine.at[block_rows(peer), :], rows.at[z, :, lanes(c)],
            x_send.at[peer], x_recv.at[c], {"cent": peer},
        )

    def features_from(peer):
        return remote(
            fine.at[block_rows(peer), :], rows.at[z, :, lanes(peer)],
            x_send.at[peer], x_recv.at[peer], {"cent": peer},
        )

    for j in range(1, m):
        features_to(cent_peer(j)).start()
    for copy in copies:
        copy.wait()

    scale_row = jnp.zeros((1, points), jnp.float32)
    shard = lax.broadcasted_iota(jnp.int32, (1, points), 1) // SHARD
    for i in range(scales.shape[1]):
        scale_row = jnp.where(shard == i, scales[0:1, i : i + 1], scale_row)

    score = scale_row * row_dot(coarse[...], codes[...]) - half_square(coarse[...])
    expo = jnp.exp(score - jnp.max(score, axis=0, keepdims=True))
    resp[...] = expo / jnp.sum(expo, axis=0, keepdims=True)
    slots = lists.shape[1]
    shape = (slots, slots)
    slot = lax.broadcasted_iota(jnp.int32, shape, 1)
    named = jnp.logical_and(
        lists[...] == lax.broadcasted_iota(jnp.int32, shape, 0), slot < counts[...]
    )
    live = jnp.sum(jnp.where(named, 1.0, 0.0), axis=1, keepdims=True) > 0.0
    parent = jnp.where(live, score[:slots], MASK_SCORE)
    parent = jnp.exp(parent - jnp.max(parent, axis=0, keepdims=True))
    parent = jnp.where(live, parent, 0.0)
    prior[...] = parent / jnp.sum(parent, axis=0, keepdims=True)

    def half_copy(b, h, send, target):
        part_of = rows.at[b, pl.ds(h * half, half), :]
        return remote(part_of, part_of, send.at[b, h], g_recv.at[b, h], {"pts": target})

    def to_right(b, h):
        return half_copy(b, h, gr_send, right)

    def to_left(b, h):
        return half_copy(b, h, gl_send, left)

    def pass_on(d):
        for h in range(HALVES):
            @pl.when(z - d >= 0)
            def _():
                to_right(z - d, h).wait_recv()

                @pl.when(z < n - 1)
                def _():
                    to_right(z - d, h).start()

            @pl.when(z + d < n)
            def _():
                to_left(z + d, h).wait_recv()

                @pl.when(z > 0)
                def _():
                    to_left(z + d, h).start()

    for j in range(1, m):
        features_from(cent_peer(j)).wait_recv()
    for h in range(HALVES):
        @pl.when(z < n - 1)
        def _():
            to_right(z, h).start()

        @pl.when(z > 0)
        def _():
            to_left(z, h).start()

    mine = resp[pl.ds(pl.multiple_of(c * share, share), share), :]
    coarse_part = jnp.dot(
        (mine * scale_row).astype(jnp.bfloat16), codes[...], preferred_element_type=jnp.float32
    )
    coarse_own[...] = coarse_part
    coarse_out[...] = coarse_part.astype(jnp.bfloat16)
    coarse_mass[z] = to_row(jnp.sum(mine, axis=1, keepdims=True))

    def piece_rows(i):
        return pl.ds(pl.multiple_of(i * piece, piece), piece)

    def piece_to(peer):
        return remote(
            coarse_out.at[piece_rows(peer), :], coarse_in_sums.at[z],
            cs_send.at[peer], cs_recv.at[z], {"pts": peer},
        )

    def piece_from(peer):
        return remote(
            coarse_out.at[piece_rows(peer), :], coarse_in_sums.at[peer],
            cs_send.at[peer], cs_recv.at[peer], {"pts": peer},
        )

    def new_to(peer):
        return remote(
            coarse_new.at[z], coarse_new.at[z], cg_send.at[peer], cg_recv.at[z], {"pts": peer}
        )

    def new_from(peer):
        return remote(
            coarse_new.at[peer], coarse_new.at[peer], cg_send.at[peer], cg_recv.at[peer],
            {"pts": peer},
        )

    def coarse_mass_to(peer):
        return remote(
            coarse_mass.at[z], coarse_mass.at[z], cm_send.at[peer], cm_recv.at[z], {"pts": peer}
        )

    def coarse_mass_from(peer):
        return remote(
            coarse_mass.at[peer], coarse_mass.at[peer], cm_send.at[peer], cm_recv.at[peer],
            {"pts": peer},
        )

    for j in range(1, n):
        coarse_mass_to(pts_peer(j)).start()
        piece_to(pts_peer(j)).start()

    def mass_to(peer):
        return remote(
            mass_out.at[peer], mass_in.at[z], m_send.at[peer], m_recv.at[z], {"pts": peer}
        )

    def mass_from(peer):
        return remote(
            mass_out.at[peer], mass_in.at[peer], m_send.at[peer], m_recv.at[peer], {"pts": peer}
        )

    def use_block(b):
        block = rows[b]
        score = scale_row * row_dot(block, codes[...]) - half_square(block)
        expo = jnp.exp(score - jnp.max(score, axis=0, keepdims=True))
        factor = prior[pl.ds(b * m + c, 1), :] / jnp.sum(expo, axis=0, keepdims=True)
        share_of = expo * factor
        total = jnp.dot(
            (share_of * scale_row).astype(jnp.bfloat16), codes[...],
            preferred_element_type=jnp.float32,
        )
        return total, to_row(jnp.sum(share_of, axis=1, keepdims=True))

    def sums_to(peer):
        return remote(
            outgoing.at[peer], incoming.at[z], s_send.at[peer], s_recv.at[z], {"pts": peer}
        )

    def sums_from(peer):
        return remote(
            outgoing.at[peer], incoming.at[peer], s_send.at[peer], s_recv.at[peer], {"pts": peer}
        )

    def use_and_send(b):
        total, mass = use_block(b)
        outgoing[b] = total.astype(jnp.bfloat16)
        mass_out[b] = mass
        sums_to(b).start()
        mass_to(b).start()

    def finish_coarse_piece():
        total = coarse_own[piece_rows(z), :]
        mass = coarse_mass[z]
        for j in range(1, n):
            peer = pts_peer(j)
            coarse_mass_from(peer).wait_recv()
            piece_from(peer).wait_recv()
            total = total + coarse_in_sums[peer].astype(jnp.float32)
            mass = mass + coarse_mass[peer]
        own = coarse[pl.ds(pl.multiple_of(c * share + z * piece, piece), piece), :]
        new = (total + PRIOR_MASS * own.astype(jnp.float32)) / (
            to_column(mass[0:1], piece, z * piece) + PRIOR_MASS
        )
        coarse_new[z] = new.astype(jnp.bfloat16)
        for j in range(1, n):
            new_to(pts_peer(j)).start()

    own_part[...], mass_in[z] = use_block(z)
    for d in range(1, n):
        pass_on(d)

        @pl.when(z - d >= 0)
        def _():
            use_and_send(z - d)

        @pl.when(z + d < n)
        def _():
            use_and_send(z + d)

        if d == 1:
            finish_coarse_piece()

    total = own_part[...] + PRIOR_MASS * rows[z].astype(jnp.float32)
    mass = mass_in[z]
    for j in range(1, n):
        peer = pts_peer(j)
        mass_from(peer).wait_recv()
        sums_from(peer).wait_recv()
        total = total + incoming[peer].astype(jnp.float32)
        mass = mass + mass_in[peer]
    new = total / (to_column(mass[0:1], BLOCK) + PRIOR_MASS)
    own_part[...] = new
    finished[...] = new.astype(jnp.bfloat16)

    def result_to(peer):
        return remote(
            finished.at[:, lanes(peer)], arrived.at[c], o_send.at[peer], o_recv.at[c],
            {"cent": peer},
        )

    def result_from(peer):
        return remote(
            finished.at[:, lanes(peer)], arrived.at[peer], o_send.at[peer], o_recv.at[peer],
            {"cent": peer},
        )

    for j in range(1, m):
        result_to(cent_peer(j)).start()
    out_fine[block_rows(c), :] = own_part[:, lanes(c)]

    for j in range(1, m):
        features_to(cent_peer(j)).wait_send()
    for d in range(n):
        for h in range(HALVES):
            @pl.when(jnp.logical_and(z - d >= 0, z < n - 1))
            def _():
                to_right(z - d, h).wait_send()

            @pl.when(jnp.logical_and(z + d < n, z > 0))
            def _():
                to_left(z + d, h).wait_send()

    for j in range(1, n):
        peer = pts_peer(j)
        new_from(peer).wait_recv()
        new_to(peer).wait_send()
        piece_to(peer).wait_send()
        coarse_mass_to(peer).wait_send()
        mass_to(peer).wait_send()
        sums_to(peer).wait_send()
    for i in range(n):
        out_coarse[i * piece : (i + 1) * piece, :] = coarse_new[i].astype(jnp.float32)

    for j in range(1, m):
        peer = cent_peer(j)
        result_from(peer).wait_recv()
        out_fine[block_rows(peer), :] = arrived[peer].astype(jnp.float32)
    for j in range(1, m):
        result_to(cent_peer(j)).wait_send()


def body(point_codes, shard_scales, coarse_centroids, fine_centroids, block_lists, live_counts):
    n = lax.axis_size("pts")
    m = lax.axis_size("cent")
    points, width = point_codes.shape
    own_blocks = fine_centroids.shape[0] // BLOCK
    quarter = fine_centroids.shape[1]
    slots = block_lists.shape[1]
    every_block = slots == n * own_blocks and own_blocks == m and slots <= NCOARSE
    every_block = every_block and NCOARSE % (16 * m * n) == 0
    if not every_block:
        return general_body(
            point_codes, shard_scales, coarse_centroids, fine_centroids, block_lists, live_counts
        )
    share = NCOARSE // m
    f32, bf16 = jnp.float32, jnp.bfloat16
    dma = pltpu.SemaphoreType.DMA
    vmem = pl.BlockSpec(memory_space=pltpu.VMEM)
    hbm = pl.BlockSpec(memory_space=pl.ANY)
    return pl.pallas_call(
        functools.partial(kernel, n, m),
        out_shape=(
            jax.ShapeDtypeStruct((share, width), f32),
            jax.ShapeDtypeStruct((own_blocks * BLOCK, quarter), f32),
        ),
        in_specs=[hbm, vmem, hbm, hbm, vmem, vmem],
        out_specs=(vmem, vmem),
        scratch_shapes=[
            pltpu.VMEM(point_codes.shape, bf16),
            pltpu.VMEM(coarse_centroids.shape, bf16),
            pltpu.VMEM((n, BLOCK, width), bf16),
            pltpu.VMEM((BLOCK, width), f32),
            pltpu.VMEM((n, BLOCK, width), bf16),
            pltpu.VMEM((n, BLOCK, width), bf16),
            pltpu.VMEM((slots, points), f32),
            pltpu.VMEM((NCOARSE, points), f32),
            pltpu.VMEM((share, width), bf16),
            pltpu.VMEM((share, width), f32),
            pltpu.VMEM((n, share // n, width), bf16),
            pltpu.VMEM((n, share // n, width), bf16),
            pltpu.VMEM((n, 8, 128), f32),
            pltpu.VMEM((n, 8, 128), f32),
            pltpu.VMEM((n, 8, 128), f32),
            pltpu.VMEM((BLOCK, width), bf16),
            pltpu.VMEM((m, BLOCK, quarter), bf16),
            dma((3,)),
        ]
        + [dma((m,))] * 2
        + [dma((n, HALVES))] * 3
        + [dma((n,))] * 10
        + [dma((m,))] * 2,
        compiler_params=pltpu.CompilerParams(
            collective_id=0, has_side_effects=True, vmem_limit_bytes=60 * 1024 * 1024
        ),
    )(
        point_codes,
        shard_scales.reshape(1, -1),
        coarse_centroids,
        fine_centroids,
        block_lists,
        live_counts.reshape(1, 1),
    )


def solution(mesh):
    return jax.shard_map(
        body,
        mesh=mesh,
        in_specs=(
            P(("groups", "pts"), None),
            P(("groups", "pts")),
            P("groups", None),
            P(("groups", "pts"), "cent"),
            P(("groups", "pts"), None),
            P(("groups", "pts")),
        ),
        out_specs=(P(("groups", "cent"), None), P(("groups", "pts"), "cent")),
        check_vma=False,
    )
```

```python
import functools

import jax
import jax.numpy as jnp
from jax import lax
from jax.experimental import pallas as pl
from jax.experimental.pallas import tpu as pltpu
from jax.sharding import PartitionSpec as P

NCOARSE = 256
BLOCK = 64
SHARD = 256


PRIOR_MASS = 1.0
MASK_SCORE = -1e30
HALVES = 2


def joined(part, axis, combine):
    gathered = jax.tree.map(lambda a: lax.all_gather(a, axis), part)

    def take(source):
        return jax.tree.map(lambda a: lax.dynamic_index_in_dim(a, source, 0, False), gathered)

    return lax.fori_loop(
        1, lax.axis_size(axis), lambda source, state: combine(state, take(source)), take(0)
    )


def combine_norms(first_part, second_part):
    peak_value = jnp.maximum(first_part[0], second_part[0])
    scaled = first_part[1] * jnp.exp(first_part[0] - peak_value) + second_part[1] * jnp.exp(
        second_part[0] - peak_value
    )
    return (peak_value, scaled)


def rank_within(owner_ids):
    width_n = owner_ids.shape[-1]
    earlier_mask = jnp.arange(width_n)[None, :] < jnp.arange(width_n)[:, None]
    same_owner = owner_ids[..., :, None] == owner_ids[..., None, :]
    return jnp.sum(jnp.logical_and(same_owner, earlier_mask), axis=-1)


def owner_selection(owner_ids, local_index, chosen, pair_slots, own_blocks):
    rank_values = rank_within(owner_ids)
    by_rank = jnp.logical_and(
        chosen[..., None], rank_values[..., None] == jnp.arange(pair_slots)
    ).astype(jnp.float32)
    by_block = (local_index[..., None] == jnp.arange(own_blocks)).astype(jnp.float32)
    return jnp.einsum("psr,psl->prl", by_rank, by_block).reshape(-1, own_blocks)


def general_body(point_codes, shard_scales, coarse_centroids, fine_centroids, block_lists, live_counts):
    pts_count = lax.axis_size("pts")
    cent_count = lax.axis_size("cent")
    pts_index = lax.axis_index("pts")
    cent_index = lax.axis_index("cent")
    point_count, width_d = point_codes.shape
    own_blocks = fine_centroids.shape[0] // BLOCK
    quarter = fine_centroids.shape[1]
    capacity = block_lists.shape[1]
    my_slots = capacity // cent_count
    pair_slots = max(1, capacity // pts_count)
    row_scale = jnp.repeat(shard_scales, SHARD)
    all_lists = lax.all_gather(block_lists, "pts", axis=0, tiled=True)
    coarse_share = NCOARSE // cent_count
    coarse_mine = lax.dynamic_slice_in_dim(
        coarse_centroids, cent_index * coarse_share, coarse_share, 0
    )
    half_mine = 0.5 * jnp.sum(jnp.square(coarse_mine.astype(jnp.float32)), axis=1)
    coarse_score = (
        row_scale[:, None]
        * jnp.einsum("pd,kd->pk", point_codes, coarse_mine, preferred_element_type=jnp.float32)
        - half_mine[None, :]
    )
    local_peak = jnp.max(coarse_score, axis=1)
    local_total = jnp.sum(jnp.exp(coarse_score - local_peak[:, None]), axis=1)
    coarse_peak, coarse_total = joined((local_peak, local_total), "cent", combine_norms)
    coarse_resp = jnp.exp(coarse_score - coarse_peak[:, None]) / coarse_total[:, None]
    coarse_weight = (coarse_resp * row_scale[:, None]).astype(jnp.bfloat16)
    coarse_sum = jnp.einsum(
        "pk,pd->kd", coarse_weight, point_codes, preferred_element_type=jnp.float32
    )
    coarse_mass = jnp.sum(coarse_resp, axis=0)
    coarse_sum, coarse_mass = lax.psum((coarse_sum, coarse_mass), "pts")
    new_coarse = (coarse_sum + PRIOR_MASS * coarse_mine.astype(jnp.float32)) / (
        coarse_mass[:, None] + PRIOR_MASS
    )
    row_list = block_lists[0]
    row_owner = row_list // own_blocks
    row_position = row_owner * pair_slots + rank_within(row_owner)
    list_owner = all_lists // own_blocks
    list_local = all_lists % own_blocks
    return_picks = owner_selection(
        list_owner, list_local, list_owner == pts_index, pair_slots, own_blocks
    )
    my_start = cent_index * my_slots
    my_blocks = lax.dynamic_slice_in_dim(row_list, my_start, my_slots, 0)
    whole_rows = lax.all_gather(fine_centroids, "cent", axis=1, tiled=True)
    in_range = jnp.arange(capacity) // my_slots == cent_index
    owner_masked = jnp.where(in_range[None, :], list_owner, -1)
    selection = owner_selection(
        owner_masked, list_local, owner_masked == pts_index, pair_slots, own_blocks
    )
    outgoing = jnp.dot(
        selection.astype(jnp.bfloat16),
        whole_rows.reshape(own_blocks, BLOCK * width_d),
        preferred_element_type=jnp.bfloat16,
    )
    arrived = lax.all_to_all(
        outgoing.reshape(pts_count * pair_slots, BLOCK, width_d),
        "pts",
        split_axis=0,
        concat_axis=0,
        tiled=True,
    )
    my_owner = my_blocks // own_blocks
    my_position = my_owner * pair_slots + rank_within(my_owner)
    block_rows = jnp.take(arrived, my_position, axis=0)
    block_flat = block_rows.reshape(my_slots * BLOCK, width_d)
    half_fine = 0.5 * jnp.sum(jnp.square(block_flat.astype(jnp.float32)), axis=1).reshape(
        my_slots, BLOCK
    )
    fine_score = row_scale[:, None] * jnp.einsum(
        "pd,jd->pj", point_codes, block_flat, preferred_element_type=jnp.float32
    )
    fine_score = fine_score.reshape(point_count, my_slots, BLOCK) - half_fine[None]
    block_peak = jnp.max(fine_score, axis=2, keepdims=True)
    block_norm = block_peak + jnp.log(
        jnp.sum(jnp.exp(fine_score - block_peak), axis=2, keepdims=True)
    )
    parent_rows = jnp.take(coarse_centroids, my_blocks % NCOARSE, axis=0)
    parent_half = 0.5 * jnp.sum(jnp.square(parent_rows.astype(jnp.float32)), axis=1)
    parent_score = (
        row_scale[:, None]
        * jnp.einsum("pd,sd->ps", point_codes, parent_rows, preferred_element_type=jnp.float32)
        - parent_half[None, :]
    )
    joint_score = parent_score[:, :, None] + fine_score - block_norm
    live_slot = my_start + jnp.arange(my_slots) < live_counts[0]
    joint_score = jnp.where(live_slot[None, :, None], joint_score, MASK_SCORE).reshape(
        point_count, my_slots * BLOCK
    )
    joint_peak = jnp.max(joint_score, axis=1)
    joint_total = jnp.sum(jnp.exp(joint_score - joint_peak[:, None]), axis=1)
    fine_peak, fine_total = joined((joint_peak, joint_total), "cent", combine_norms)
    fine_resp = jnp.exp(joint_score - fine_peak[:, None]) / fine_total[:, None]
    fine_weight = (fine_resp * row_scale[:, None]).astype(jnp.bfloat16)
    fine_sum = jnp.einsum(
        "pj,pd->jd", fine_weight, point_codes, preferred_element_type=jnp.float32
    ).reshape(my_slots, BLOCK, width_d)
    fine_mass = jnp.sum(fine_resp, axis=0).reshape(my_slots, BLOCK)
    mass_copies = jnp.broadcast_to(fine_mass[:, :, None], (my_slots, BLOCK, cent_count))
    sum_quarters, mass_quarters = (
        lax.all_to_all(fine_sum, "cent", split_axis=2, concat_axis=0, tiled=True),
        lax.all_to_all(mass_copies, "cent", split_axis=2, concat_axis=0, tiled=True),
    )
    targets = jnp.arange(pts_count * pair_slots)
    matches = row_position[None, :] == targets[:, None]
    source = jnp.sum(jnp.where(matches, jnp.arange(capacity)[None, :], 0), axis=1)
    present = jnp.any(matches, axis=1)[:, None, None]
    send_sums = jnp.where(present, jnp.take(sum_quarters, source, axis=0), 0.0)
    send_mass = jnp.where(present, jnp.take(mass_quarters, source, axis=0), 0.0)
    back_sums, back_mass = (
        lax.all_to_all(send_sums, "pts", split_axis=0, concat_axis=0, tiled=True),
        lax.all_to_all(send_mass, "pts", split_axis=0, concat_axis=0, tiled=True),
    )
    owner_sums = jnp.einsum("xl,xbq->lbq", return_picks, back_sums, precision=lax.Precision.HIGHEST)
    owner_mass = jnp.einsum("xl,xbq->lbq", return_picks, back_mass, precision=lax.Precision.HIGHEST)
    prior_rows = fine_centroids.astype(jnp.float32).reshape(own_blocks, BLOCK, quarter)
    new_fine = (owner_sums + PRIOR_MASS * prior_rows) / (owner_mass + PRIOR_MASS)
    return (new_coarse, new_fine.reshape(own_blocks * BLOCK, quarter))


def row_dot(a, b):
    return lax.dot_general(a, b, (((1,), (1,)), ((), ())), preferred_element_type=jnp.float32)


def half_square(a):
    a = a.astype(jnp.float32)
    return 0.5 * jnp.sum(a * a, axis=1, keepdims=True)


def diagonal(rows, start=0):
    shape = (rows, 128)
    row = lax.broadcasted_iota(jnp.int32, shape, 0) + start
    return row == lax.broadcasted_iota(jnp.int32, shape, 1)


def to_row(column):
    row = jnp.sum(jnp.where(diagonal(column.shape[0]), column, 0.0), axis=0, keepdims=True)
    return jnp.broadcast_to(row, (8, 128))


def to_column(row, rows, start=0):
    return jnp.sum(jnp.where(diagonal(rows, start), row, 0.0), axis=1, keepdims=True)


def kernel(
    n, m,
    codes_in, scales, coarse_in, fine, lists, counts,
    out_coarse, out_fine,
    codes, coarse, rows, own_part, outgoing, incoming, prior, resp,
    coarse_out, coarse_own, coarse_in_sums, coarse_new,
    coarse_mass, mass_out, mass_in, finished, arrived,
    in_sem, x_send, x_recv, gr_send, gl_send, g_recv,
    cs_send, cs_recv, cg_send, cg_recv,
    s_send, s_recv, m_send, m_recv, cm_send, cm_recv, o_send, o_recv,
):
    z = lax.axis_index("pts")
    c = lax.axis_index("cent")
    right, left = lax.rem(z + 1, n), lax.rem(z + n - 1, n)
    points, width = codes.shape
    quarter = fine.shape[1]
    share = coarse.shape[0] // m
    piece = share // n
    half = BLOCK // HALVES

    def remote(src, dst, send, recv, target):
        return pltpu.make_async_remote_copy(
            src_ref=src, dst_ref=dst, send_sem=send, recv_sem=recv,
            device_id=target, device_id_type=pl.DeviceIdType.MESH,
        )

    def cent_peer(j):
        return lax.rem(c + j, m)

    def pts_peer(j):
        return lax.rem(z + j, n)

    def lanes(i):
        return pl.ds(pl.multiple_of(i * quarter, quarter), quarter)

    def block_rows(i):
        return pl.ds(pl.multiple_of(i * BLOCK, BLOCK), BLOCK)

    barrier = pltpu.get_barrier_semaphore()
    copies = [
        pltpu.make_async_copy(coarse_in, coarse, in_sem.at[0]),
        pltpu.make_async_copy(codes_in, codes, in_sem.at[1]),
        pltpu.make_async_copy(fine.at[block_rows(c), :], rows.at[z, :, lanes(c)], in_sem.at[2]),
    ]
    for j in range(1, m):
        pl.semaphore_signal(
            barrier, inc=1, device_id={"cent": cent_peer(j)}, device_id_type=pl.DeviceIdType.MESH
        )
    for j in range(1, n):
        pl.semaphore_signal(
            barrier, inc=1, device_id={"pts": pts_peer(j)}, device_id_type=pl.DeviceIdType.MESH
        )
    for copy in copies:
        copy.start()
    pl.semaphore_wait(barrier, n + m - 2)

    def features_to(peer):
        return remote(
            fine.at[block_rows(peer), :], rows.at[z, :, lanes(c)],
            x_send.at[peer], x_recv.at[c], {"cent": peer},
        )

    def features_from(peer):
        return remote(
            fine.at[block_rows(peer), :], rows.at[z, :, lanes(peer)],
            x_send.at[peer], x_recv.at[peer], {"cent": peer},
        )

    for j in range(1, m):
        features_to(cent_peer(j)).start()
    for copy in copies:
        copy.wait()

    scale_row = jnp.zeros((1, points), jnp.float32)
    shard = lax.broadcasted_iota(jnp.int32, (1, points), 1) // SHARD
    for i in range(scales.shape[1]):
        scale_row = jnp.where(shard == i, scales[0:1, i : i + 1], scale_row)

    score = scale_row * row_dot(coarse[...], codes[...]) - half_square(coarse[...])
    expo = jnp.exp(score - jnp.max(score, axis=0, keepdims=True))
    resp[...] = expo / jnp.sum(expo, axis=0, keepdims=True)
    slots = lists.shape[1]
    shape = (slots, slots)
    slot = lax.broadcasted_iota(jnp.int32, shape, 1)
    named = jnp.logical_and(
        lists[...] == lax.broadcasted_iota(jnp.int32, shape, 0), slot < counts[...]
    )
    live = jnp.sum(jnp.where(named, 1.0, 0.0), axis=1, keepdims=True) > 0.0
    parent = jnp.where(live, score[:slots], MASK_SCORE)
    parent = jnp.exp(parent - jnp.max(parent, axis=0, keepdims=True))
    parent = jnp.where(live, parent, 0.0)
    prior[...] = parent / jnp.sum(parent, axis=0, keepdims=True)

    def half_copy(b, h, send, target):
        part_of = rows.at[b, pl.ds(h * half, half), :]
        return remote(part_of, part_of, send.at[b, h], g_recv.at[b, h], {"pts": target})

    def to_right(b, h):
        return half_copy(b, h, gr_send, right)

    def to_left(b, h):
        return half_copy(b, h, gl_send, left)

    def pass_on(d):
        for h in range(HALVES):
            @pl.when(z - d >= 0)
            def _():
                to_right(z - d, h).wait_recv()

                @pl.when(z < n - 1)
                def _():
                    to_right(z - d, h).start()

            @pl.when(z + d < n)
            def _():
                to_left(z + d, h).wait_recv()

                @pl.when(z > 0)
                def _():
                    to_left(z + d, h).start()

    for j in range(1, m):
        features_from(cent_peer(j)).wait_recv()
    for h in range(HALVES):
        @pl.when(z < n - 1)
        def _():
            to_right(z, h).start()

        @pl.when(z > 0)
        def _():
            to_left(z, h).start()

    mine = resp[pl.ds(pl.multiple_of(c * share, share), share), :]
    coarse_part = jnp.dot(
        (mine * scale_row).astype(jnp.bfloat16), codes[...], preferred_element_type=jnp.float32
    )
    coarse_own[...] = coarse_part
    coarse_out[...] = coarse_part.astype(jnp.bfloat16)
    coarse_mass[z] = to_row(jnp.sum(mine, axis=1, keepdims=True))

    def piece_rows(i):
        return pl.ds(pl.multiple_of(i * piece, piece), piece)

    def piece_to(peer):
        return remote(
            coarse_out.at[piece_rows(peer), :], coarse_in_sums.at[z],
            cs_send.at[peer], cs_recv.at[z], {"pts": peer},
        )

    def piece_from(peer):
        return remote(
            coarse_out.at[piece_rows(peer), :], coarse_in_sums.at[peer],
            cs_send.at[peer], cs_recv.at[peer], {"pts": peer},
        )

    def new_to(peer):
        return remote(
            coarse_new.at[z], coarse_new.at[z], cg_send.at[peer], cg_recv.at[z], {"pts": peer}
        )

    def new_from(peer):
        return remote(
            coarse_new.at[peer], coarse_new.at[peer], cg_send.at[peer], cg_recv.at[peer],
            {"pts": peer},
        )

    def coarse_mass_to(peer):
        return remote(
            coarse_mass.at[z], coarse_mass.at[z], cm_send.at[peer], cm_recv.at[z], {"pts": peer}
        )

    def coarse_mass_from(peer):
        return remote(
            coarse_mass.at[peer], coarse_mass.at[peer], cm_send.at[peer], cm_recv.at[peer],
            {"pts": peer},
        )

    for j in range(1, n):
        coarse_mass_to(pts_peer(j)).start()
        piece_to(pts_peer(j)).start()

    def mass_to(peer):
        return remote(
            mass_out.at[peer], mass_in.at[z], m_send.at[peer], m_recv.at[z], {"pts": peer}
        )

    def mass_from(peer):
        return remote(
            mass_out.at[peer], mass_in.at[peer], m_send.at[peer], m_recv.at[peer], {"pts": peer}
        )

    def use_block(b):
        block = rows[b]
        score = scale_row * row_dot(block, codes[...]) - half_square(block)
        expo = jnp.exp(score - jnp.max(score, axis=0, keepdims=True))
        factor = prior[pl.ds(b * m + c, 1), :] / jnp.sum(expo, axis=0, keepdims=True)
        share_of = expo * factor
        total = jnp.dot(
            (share_of * scale_row).astype(jnp.bfloat16), codes[...],
            preferred_element_type=jnp.float32,
        )
        return total, to_row(jnp.sum(share_of, axis=1, keepdims=True))

    def sums_to(peer):
        return remote(
            outgoing.at[peer], incoming.at[z], s_send.at[peer], s_recv.at[z], {"pts": peer}
        )

    def sums_from(peer):
        return remote(
            outgoing.at[peer], incoming.at[peer], s_send.at[peer], s_recv.at[peer], {"pts": peer}
        )

    def use_and_send(b):
        total, mass = use_block(b)
        outgoing[b] = total.astype(jnp.bfloat16)
        mass_out[b] = mass
        sums_to(b).start()
        mass_to(b).start()

    def finish_coarse_piece():
        total = coarse_own[piece_rows(z), :]
        mass = coarse_mass[z]
        for j in range(1, n):
            peer = pts_peer(j)
            coarse_mass_from(peer).wait_recv()
            piece_from(peer).wait_recv()
            total = total + coarse_in_sums[peer].astype(jnp.float32)
            mass = mass + coarse_mass[peer]
        own = coarse[pl.ds(pl.multiple_of(c * share + z * piece, piece), piece), :]
        new = (total + PRIOR_MASS * own.astype(jnp.float32)) / (
            to_column(mass[0:1], piece, z * piece) + PRIOR_MASS
        )
        coarse_new[z] = new.astype(jnp.bfloat16)
        for j in range(1, n):
            new_to(pts_peer(j)).start()

    own_part[...], mass_in[z] = use_block(z)
    for d in range(1, n):
        pass_on(d)

        @pl.when(z - d >= 0)
        def _():
            use_and_send(z - d)

        @pl.when(z + d < n)
        def _():
            use_and_send(z + d)

        if d == max(1, n - 2):
            finish_coarse_piece()

    total = own_part[...] + PRIOR_MASS * rows[z].astype(jnp.float32)
    mass = mass_in[z]
    for j in range(1, n):
        peer = pts_peer(j)
        mass_from(peer).wait_recv()
        sums_from(peer).wait_recv()
        total = total + incoming[peer].astype(jnp.float32)
        mass = mass + mass_in[peer]
    new = total / (to_column(mass[0:1], BLOCK) + PRIOR_MASS)
    own_part[...] = new
    finished[...] = new.astype(jnp.bfloat16)

    def result_to(peer):
        return remote(
            finished.at[:, lanes(peer)], arrived.at[c], o_send.at[peer], o_recv.at[c],
            {"cent": peer},
        )

    def result_from(peer):
        return remote(
            finished.at[:, lanes(peer)], arrived.at[peer], o_send.at[peer], o_recv.at[peer],
            {"cent": peer},
        )

    for j in range(1, m):
        result_to(cent_peer(j)).start()
    out_fine[block_rows(c), :] = own_part[:, lanes(c)]

    for j in range(1, m):
        features_to(cent_peer(j)).wait_send()
    for d in range(n):
        for h in range(HALVES):
            @pl.when(jnp.logical_and(z - d >= 0, z < n - 1))
            def _():
                to_right(z - d, h).wait_send()

            @pl.when(jnp.logical_and(z + d < n, z > 0))
            def _():
                to_left(z + d, h).wait_send()

    for j in range(1, n):
        peer = pts_peer(j)
        new_from(peer).wait_recv()
        new_to(peer).wait_send()
        piece_to(peer).wait_send()
        coarse_mass_to(peer).wait_send()
        mass_to(peer).wait_send()
        sums_to(peer).wait_send()
    for i in range(n):
        out_coarse[i * piece : (i + 1) * piece, :] = coarse_new[i].astype(jnp.float32)

    for j in range(1, m):
        peer = cent_peer(j)
        result_from(peer).wait_recv()
        out_fine[block_rows(peer), :] = arrived[peer].astype(jnp.float32)
    for j in range(1, m):
        result_to(cent_peer(j)).wait_send()


def body(point_codes, shard_scales, coarse_centroids, fine_centroids, block_lists, live_counts):
    n = lax.axis_size("pts")
    m = lax.axis_size("cent")
    points, width = point_codes.shape
    own_blocks = fine_centroids.shape[0] // BLOCK
    quarter = fine_centroids.shape[1]
    slots = block_lists.shape[1]
    every_block = slots == n * own_blocks and own_blocks == m and slots <= NCOARSE
    every_block = every_block and NCOARSE % (16 * m * n) == 0
    if not every_block:
        return general_body(
            point_codes, shard_scales, coarse_centroids, fine_centroids, block_lists, live_counts
        )
    share = NCOARSE // m
    f32, bf16 = jnp.float32, jnp.bfloat16
    dma = pltpu.SemaphoreType.DMA
    vmem = pl.BlockSpec(memory_space=pltpu.VMEM)
    hbm = pl.BlockSpec(memory_space=pl.ANY)
    return pl.pallas_call(
        functools.partial(kernel, n, m),
        out_shape=(
            jax.ShapeDtypeStruct((share, width), f32),
            jax.ShapeDtypeStruct((own_blocks * BLOCK, quarter), f32),
        ),
        in_specs=[hbm, vmem, hbm, hbm, vmem, vmem],
        out_specs=(vmem, vmem),
        scratch_shapes=[
            pltpu.VMEM(point_codes.shape, bf16),
            pltpu.VMEM(coarse_centroids.shape, bf16),
            pltpu.VMEM((n, BLOCK, width), bf16),
            pltpu.VMEM((BLOCK, width), f32),
            pltpu.VMEM((n, BLOCK, width), bf16),
            pltpu.VMEM((n, BLOCK, width), bf16),
            pltpu.VMEM((slots, points), f32),
            pltpu.VMEM((NCOARSE, points), f32),
            pltpu.VMEM((share, width), bf16),
            pltpu.VMEM((share, width), f32),
            pltpu.VMEM((n, share // n, width), bf16),
            pltpu.VMEM((n, share // n, width), bf16),
            pltpu.VMEM((n, 8, 128), f32),
            pltpu.VMEM((n, 8, 128), f32),
            pltpu.VMEM((n, 8, 128), f32),
            pltpu.VMEM((BLOCK, width), bf16),
            pltpu.VMEM((m, BLOCK, quarter), bf16),
            dma((3,)),
        ]
        + [dma((m,))] * 2
        + [dma((n, HALVES))] * 3
        + [dma((n,))] * 10
        + [dma((m,))] * 2,
        compiler_params=pltpu.CompilerParams(
            collective_id=0, has_side_effects=True, vmem_limit_bytes=60 * 1024 * 1024
        ),
    )(
        point_codes,
        shard_scales.reshape(1, -1),
        coarse_centroids,
        fine_centroids,
        block_lists,
        live_counts.reshape(1, 1),
    )


def solution(mesh):
    return jax.shard_map(
        body,
        mesh=mesh,
        in_specs=(
            P(("groups", "pts"), None),
            P(("groups", "pts")),
            P("groups", None),
            P(("groups", "pts"), "cent"),
            P(("groups", "pts"), None),
            P(("groups", "pts")),
        ),
        out_specs=(P(("groups", "cent"), None), P(("groups", "pts"), "cent")),
        check_vma=False,
    )
```

```python
import functools

import jax
import jax.numpy as jnp
from jax import lax
from jax.experimental import pallas as pl
from jax.experimental.pallas import tpu as pltpu
from jax.sharding import PartitionSpec as P

NCOARSE = 256
BLOCK = 64
SHARD = 256


PRIOR_MASS = 1.0
MASK_SCORE = -1e30
HALVES = 4


def joined(part, axis, combine):
    gathered = jax.tree.map(lambda a: lax.all_gather(a, axis), part)

    def take(source):
        return jax.tree.map(lambda a: lax.dynamic_index_in_dim(a, source, 0, False), gathered)

    return lax.fori_loop(
        1, lax.axis_size(axis), lambda source, state: combine(state, take(source)), take(0)
    )


def combine_norms(first_part, second_part):
    peak_value = jnp.maximum(first_part[0], second_part[0])
    scaled = first_part[1] * jnp.exp(first_part[0] - peak_value) + second_part[1] * jnp.exp(
        second_part[0] - peak_value
    )
    return (peak_value, scaled)


def rank_within(owner_ids):
    width_n = owner_ids.shape[-1]
    earlier_mask = jnp.arange(width_n)[None, :] < jnp.arange(width_n)[:, None]
    same_owner = owner_ids[..., :, None] == owner_ids[..., None, :]
    return jnp.sum(jnp.logical_and(same_owner, earlier_mask), axis=-1)


def owner_selection(owner_ids, local_index, chosen, pair_slots, own_blocks):
    rank_values = rank_within(owner_ids)
    by_rank = jnp.logical_and(
        chosen[..., None], rank_values[..., None] == jnp.arange(pair_slots)
    ).astype(jnp.float32)
    by_block = (local_index[..., None] == jnp.arange(own_blocks)).astype(jnp.float32)
    return jnp.einsum("psr,psl->prl", by_rank, by_block).reshape(-1, own_blocks)


def general_body(point_codes, shard_scales, coarse_centroids, fine_centroids, block_lists, live_counts):
    pts_count = lax.axis_size("pts")
    cent_count = lax.axis_size("cent")
    pts_index = lax.axis_index("pts")
    cent_index = lax.axis_index("cent")
    point_count, width_d = point_codes.shape
    own_blocks = fine_centroids.shape[0] // BLOCK
    quarter = fine_centroids.shape[1]
    capacity = block_lists.shape[1]
    my_slots = capacity // cent_count
    pair_slots = max(1, capacity // pts_count)
    row_scale = jnp.repeat(shard_scales, SHARD)
    all_lists = lax.all_gather(block_lists, "pts", axis=0, tiled=True)
    coarse_share = NCOARSE // cent_count
    coarse_mine = lax.dynamic_slice_in_dim(
        coarse_centroids, cent_index * coarse_share, coarse_share, 0
    )
    half_mine = 0.5 * jnp.sum(jnp.square(coarse_mine.astype(jnp.float32)), axis=1)
    coarse_score = (
        row_scale[:, None]
        * jnp.einsum("pd,kd->pk", point_codes, coarse_mine, preferred_element_type=jnp.float32)
        - half_mine[None, :]
    )
    local_peak = jnp.max(coarse_score, axis=1)
    local_total = jnp.sum(jnp.exp(coarse_score - local_peak[:, None]), axis=1)
    coarse_peak, coarse_total = joined((local_peak, local_total), "cent", combine_norms)
    coarse_resp = jnp.exp(coarse_score - coarse_peak[:, None]) / coarse_total[:, None]
    coarse_weight = (coarse_resp * row_scale[:, None]).astype(jnp.bfloat16)
    coarse_sum = jnp.einsum(
        "pk,pd->kd", coarse_weight, point_codes, preferred_element_type=jnp.float32
    )
    coarse_mass = jnp.sum(coarse_resp, axis=0)
    coarse_sum, coarse_mass = lax.psum((coarse_sum, coarse_mass), "pts")
    new_coarse = (coarse_sum + PRIOR_MASS * coarse_mine.astype(jnp.float32)) / (
        coarse_mass[:, None] + PRIOR_MASS
    )
    row_list = block_lists[0]
    row_owner = row_list // own_blocks
    row_position = row_owner * pair_slots + rank_within(row_owner)
    list_owner = all_lists // own_blocks
    list_local = all_lists % own_blocks
    return_picks = owner_selection(
        list_owner, list_local, list_owner == pts_index, pair_slots, own_blocks
    )
    my_start = cent_index * my_slots
    my_blocks = lax.dynamic_slice_in_dim(row_list, my_start, my_slots, 0)
    whole_rows = lax.all_gather(fine_centroids, "cent", axis=1, tiled=True)
    in_range = jnp.arange(capacity) // my_slots == cent_index
    owner_masked = jnp.where(in_range[None, :], list_owner, -1)
    selection = owner_selection(
        owner_masked, list_local, owner_masked == pts_index, pair_slots, own_blocks
    )
    outgoing = jnp.dot(
        selection.astype(jnp.bfloat16),
        whole_rows.reshape(own_blocks, BLOCK * width_d),
        preferred_element_type=jnp.bfloat16,
    )
    arrived = lax.all_to_all(
        outgoing.reshape(pts_count * pair_slots, BLOCK, width_d),
        "pts",
        split_axis=0,
        concat_axis=0,
        tiled=True,
    )
    my_owner = my_blocks // own_blocks
    my_position = my_owner * pair_slots + rank_within(my_owner)
    block_rows = jnp.take(arrived, my_position, axis=0)
    block_flat = block_rows.reshape(my_slots * BLOCK, width_d)
    half_fine = 0.5 * jnp.sum(jnp.square(block_flat.astype(jnp.float32)), axis=1).reshape(
        my_slots, BLOCK
    )
    fine_score = row_scale[:, None] * jnp.einsum(
        "pd,jd->pj", point_codes, block_flat, preferred_element_type=jnp.float32
    )
    fine_score = fine_score.reshape(point_count, my_slots, BLOCK) - half_fine[None]
    block_peak = jnp.max(fine_score, axis=2, keepdims=True)
    block_norm = block_peak + jnp.log(
        jnp.sum(jnp.exp(fine_score - block_peak), axis=2, keepdims=True)
    )
    parent_rows = jnp.take(coarse_centroids, my_blocks % NCOARSE, axis=0)
    parent_half = 0.5 * jnp.sum(jnp.square(parent_rows.astype(jnp.float32)), axis=1)
    parent_score = (
        row_scale[:, None]
        * jnp.einsum("pd,sd->ps", point_codes, parent_rows, preferred_element_type=jnp.float32)
        - parent_half[None, :]
    )
    joint_score = parent_score[:, :, None] + fine_score - block_norm
    live_slot = my_start + jnp.arange(my_slots) < live_counts[0]
    joint_score = jnp.where(live_slot[None, :, None], joint_score, MASK_SCORE).reshape(
        point_count, my_slots * BLOCK
    )
    joint_peak = jnp.max(joint_score, axis=1)
    joint_total = jnp.sum(jnp.exp(joint_score - joint_peak[:, None]), axis=1)
    fine_peak, fine_total = joined((joint_peak, joint_total), "cent", combine_norms)
    fine_resp = jnp.exp(joint_score - fine_peak[:, None]) / fine_total[:, None]
    fine_weight = (fine_resp * row_scale[:, None]).astype(jnp.bfloat16)
    fine_sum = jnp.einsum(
        "pj,pd->jd", fine_weight, point_codes, preferred_element_type=jnp.float32
    ).reshape(my_slots, BLOCK, width_d)
    fine_mass = jnp.sum(fine_resp, axis=0).reshape(my_slots, BLOCK)
    mass_copies = jnp.broadcast_to(fine_mass[:, :, None], (my_slots, BLOCK, cent_count))
    sum_quarters, mass_quarters = (
        lax.all_to_all(fine_sum, "cent", split_axis=2, concat_axis=0, tiled=True),
        lax.all_to_all(mass_copies, "cent", split_axis=2, concat_axis=0, tiled=True),
    )
    targets = jnp.arange(pts_count * pair_slots)
    matches = row_position[None, :] == targets[:, None]
    source = jnp.sum(jnp.where(matches, jnp.arange(capacity)[None, :], 0), axis=1)
    present = jnp.any(matches, axis=1)[:, None, None]
    send_sums = jnp.where(present, jnp.take(sum_quarters, source, axis=0), 0.0)
    send_mass = jnp.where(present, jnp.take(mass_quarters, source, axis=0), 0.0)
    back_sums, back_mass = (
        lax.all_to_all(send_sums, "pts", split_axis=0, concat_axis=0, tiled=True),
        lax.all_to_all(send_mass, "pts", split_axis=0, concat_axis=0, tiled=True),
    )
    owner_sums = jnp.einsum("xl,xbq->lbq", return_picks, back_sums, precision=lax.Precision.HIGHEST)
    owner_mass = jnp.einsum("xl,xbq->lbq", return_picks, back_mass, precision=lax.Precision.HIGHEST)
    prior_rows = fine_centroids.astype(jnp.float32).reshape(own_blocks, BLOCK, quarter)
    new_fine = (owner_sums + PRIOR_MASS * prior_rows) / (owner_mass + PRIOR_MASS)
    return (new_coarse, new_fine.reshape(own_blocks * BLOCK, quarter))


def row_dot(a, b):
    return lax.dot_general(a, b, (((1,), (1,)), ((), ())), preferred_element_type=jnp.float32)


def half_square(a):
    a = a.astype(jnp.float32)
    return 0.5 * jnp.sum(a * a, axis=1, keepdims=True)


def diagonal(rows, start=0):
    shape = (rows, 128)
    row = lax.broadcasted_iota(jnp.int32, shape, 0) + start
    return row == lax.broadcasted_iota(jnp.int32, shape, 1)


def to_row(column):
    row = jnp.sum(jnp.where(diagonal(column.shape[0]), column, 0.0), axis=0, keepdims=True)
    return jnp.broadcast_to(row, (8, 128))


def to_column(row, rows, start=0):
    return jnp.sum(jnp.where(diagonal(rows, start), row, 0.0), axis=1, keepdims=True)


def kernel(
    n, m,
    codes_in, scales, coarse_in, fine, lists, counts,
    out_coarse, out_fine,
    codes, coarse, rows, own_part, outgoing, incoming, prior, resp,
    coarse_out, coarse_own, coarse_in_sums, coarse_new,
    coarse_mass, mass_out, mass_in, finished, arrived,
    in_sem, x_send, x_recv, gr_send, gl_send, g_recv,
    cs_send, cs_recv, cg_send, cg_recv,
    s_send, s_recv, m_send, m_recv, cm_send, cm_recv, o_send, o_recv,
):
    z = lax.axis_index("pts")
    c = lax.axis_index("cent")
    right, left = lax.rem(z + 1, n), lax.rem(z + n - 1, n)
    points, width = codes.shape
    quarter = fine.shape[1]
    share = coarse.shape[0] // m
    piece = share // n
    half = BLOCK // HALVES

    def remote(src, dst, send, recv, target):
        return pltpu.make_async_remote_copy(
            src_ref=src, dst_ref=dst, send_sem=send, recv_sem=recv,
            device_id=target, device_id_type=pl.DeviceIdType.MESH,
        )

    def cent_peer(j):
        return lax.rem(c + j, m)

    def pts_peer(j):
        return lax.rem(z + j, n)

    def lanes(i):
        return pl.ds(pl.multiple_of(i * quarter, quarter), quarter)

    def block_rows(i):
        return pl.ds(pl.multiple_of(i * BLOCK, BLOCK), BLOCK)

    barrier = pltpu.get_barrier_semaphore()
    copies = [
        pltpu.make_async_copy(coarse_in, coarse, in_sem.at[0]),
        pltpu.make_async_copy(codes_in, codes, in_sem.at[1]),
        pltpu.make_async_copy(fine.at[block_rows(c), :], rows.at[z, :, lanes(c)], in_sem.at[2]),
    ]
    for j in range(1, m):
        pl.semaphore_signal(
            barrier, inc=1, device_id={"cent": cent_peer(j)}, device_id_type=pl.DeviceIdType.MESH
        )
    for j in range(1, n):
        pl.semaphore_signal(
            barrier, inc=1, device_id={"pts": pts_peer(j)}, device_id_type=pl.DeviceIdType.MESH
        )
    for copy in copies:
        copy.start()
    pl.semaphore_wait(barrier, n + m - 2)

    def features_to(peer):
        return remote(
            fine.at[block_rows(peer), :], rows.at[z, :, lanes(c)],
            x_send.at[peer], x_recv.at[c], {"cent": peer},
        )

    def features_from(peer):
        return remote(
            fine.at[block_rows(peer), :], rows.at[z, :, lanes(peer)],
            x_send.at[peer], x_recv.at[peer], {"cent": peer},
        )

    for j in range(1, m):
        features_to(cent_peer(j)).start()
    for copy in copies:
        copy.wait()

    scale_row = jnp.zeros((1, points), jnp.float32)
    shard = lax.broadcasted_iota(jnp.int32, (1, points), 1) // SHARD
    for i in range(scales.shape[1]):
        scale_row = jnp.where(shard == i, scales[0:1, i : i + 1], scale_row)

    score = scale_row * row_dot(coarse[...], codes[...]) - half_square(coarse[...])
    expo = jnp.exp(score - jnp.max(score, axis=0, keepdims=True))
    resp[...] = expo / jnp.sum(expo, axis=0, keepdims=True)
    slots = lists.shape[1]
    shape = (slots, slots)
    slot = lax.broadcasted_iota(jnp.int32, shape, 1)
    named = jnp.logical_and(
        lists[...] == lax.broadcasted_iota(jnp.int32, shape, 0), slot < counts[...]
    )
    live = jnp.sum(jnp.where(named, 1.0, 0.0), axis=1, keepdims=True) > 0.0
    parent = jnp.where(live, score[:slots], MASK_SCORE)
    parent = jnp.exp(parent - jnp.max(parent, axis=0, keepdims=True))
    parent = jnp.where(live, parent, 0.0)
    prior[...] = parent / jnp.sum(parent, axis=0, keepdims=True)

    def half_copy(b, h, send, target):
        part_of = rows.at[b, pl.ds(h * half, half), :]
        return remote(part_of, part_of, send.at[b, h], g_recv.at[b, h], {"pts": target})

    def to_right(b, h):
        return half_copy(b, h, gr_send, right)

    def to_left(b, h):
        return half_copy(b, h, gl_send, left)

    def pass_on(d):
        for h in range(HALVES):
            @pl.when(z - d >= 0)
            def _():
                to_right(z - d, h).wait_recv()

                @pl.when(z < n - 1)
                def _():
                    to_right(z - d, h).start()

            @pl.when(z + d < n)
            def _():
                to_left(z + d, h).wait_recv()

                @pl.when(z > 0)
                def _():
                    to_left(z + d, h).start()

    for j in range(1, m):
        features_from(cent_peer(j)).wait_recv()
    for h in range(HALVES):
        @pl.when(z < n - 1)
        def _():
            to_right(z, h).start()

        @pl.when(z > 0)
        def _():
            to_left(z, h).start()

    mine = resp[pl.ds(pl.multiple_of(c * share, share), share), :]
    coarse_part = jnp.dot(
        (mine * scale_row).astype(jnp.bfloat16), codes[...], preferred_element_type=jnp.float32
    )
    coarse_own[...] = coarse_part
    coarse_out[...] = coarse_part.astype(jnp.bfloat16)
    coarse_mass[z] = to_row(jnp.sum(mine, axis=1, keepdims=True))

    def piece_rows(i):
        return pl.ds(pl.multiple_of(i * piece, piece), piece)

    def piece_to(peer):
        return remote(
            coarse_out.at[piece_rows(peer), :], coarse_in_sums.at[z],
            cs_send.at[peer], cs_recv.at[z], {"pts": peer},
        )

    def piece_from(peer):
        return remote(
            coarse_out.at[piece_rows(peer), :], coarse_in_sums.at[peer],
            cs_send.at[peer], cs_recv.at[peer], {"pts": peer},
        )

    def new_to(peer):
        return remote(
            coarse_new.at[z], coarse_new.at[z], cg_send.at[peer], cg_recv.at[z], {"pts": peer}
        )

    def new_from(peer):
        return remote(
            coarse_new.at[peer], coarse_new.at[peer], cg_send.at[peer], cg_recv.at[peer],
            {"pts": peer},
        )

    def coarse_mass_to(peer):
        return remote(
            coarse_mass.at[z], coarse_mass.at[z], cm_send.at[peer], cm_recv.at[z], {"pts": peer}
        )

    def coarse_mass_from(peer):
        return remote(
            coarse_mass.at[peer], coarse_mass.at[peer], cm_send.at[peer], cm_recv.at[peer],
            {"pts": peer},
        )

    for j in range(1, n):
        coarse_mass_to(pts_peer(j)).start()
        piece_to(pts_peer(j)).start()

    def mass_to(peer):
        return remote(
            mass_out.at[peer], mass_in.at[z], m_send.at[peer], m_recv.at[z], {"pts": peer}
        )

    def mass_from(peer):
        return remote(
            mass_out.at[peer], mass_in.at[peer], m_send.at[peer], m_recv.at[peer], {"pts": peer}
        )

    def use_block(b):
        block = rows[b]
        score = scale_row * row_dot(block, codes[...]) - half_square(block)
        expo = jnp.exp(score - jnp.max(score, axis=0, keepdims=True))
        factor = prior[pl.ds(b * m + c, 1), :] / jnp.sum(expo, axis=0, keepdims=True)
        share_of = expo * factor
        total = jnp.dot(
            (share_of * scale_row).astype(jnp.bfloat16), codes[...],
            preferred_element_type=jnp.float32,
        )
        return total, to_row(jnp.sum(share_of, axis=1, keepdims=True))

    def sums_to(peer):
        return remote(
            outgoing.at[peer], incoming.at[z], s_send.at[peer], s_recv.at[z], {"pts": peer}
        )

    def sums_from(peer):
        return remote(
            outgoing.at[peer], incoming.at[peer], s_send.at[peer], s_recv.at[peer], {"pts": peer}
        )

    def use_and_send(b):
        total, mass = use_block(b)
        outgoing[b] = total.astype(jnp.bfloat16)
        mass_out[b] = mass
        sums_to(b).start()
        mass_to(b).start()

    def finish_coarse_piece():
        total = coarse_own[piece_rows(z), :]
        mass = coarse_mass[z]
        for j in range(1, n):
            peer = pts_peer(j)
            coarse_mass_from(peer).wait_recv()
            piece_from(peer).wait_recv()
            total = total + coarse_in_sums[peer].astype(jnp.float32)
            mass = mass + coarse_mass[peer]
        own = coarse[pl.ds(pl.multiple_of(c * share + z * piece, piece), piece), :]
        new = (total + PRIOR_MASS * own.astype(jnp.float32)) / (
            to_column(mass[0:1], piece, z * piece) + PRIOR_MASS
        )
        coarse_new[z] = new.astype(jnp.bfloat16)
        for j in range(1, n):
            new_to(pts_peer(j)).start()

    own_part[...], mass_in[z] = use_block(z)
    for d in range(1, n):
        pass_on(d)

        @pl.when(z - d >= 0)
        def _():
            use_and_send(z - d)

        @pl.when(z + d < n)
        def _():
            use_and_send(z + d)

        if d == max(1, n - 2):
            finish_coarse_piece()

    total = own_part[...] + PRIOR_MASS * rows[z].astype(jnp.float32)
    mass = mass_in[z]
    for j in range(1, n):
        peer = pts_peer(j)
        mass_from(peer).wait_recv()
        sums_from(peer).wait_recv()
        total = total + incoming[peer].astype(jnp.float32)
        mass = mass + mass_in[peer]
    new = total / (to_column(mass[0:1], BLOCK) + PRIOR_MASS)
    own_part[...] = new
    finished[...] = new.astype(jnp.bfloat16)

    def result_to(peer):
        return remote(
            finished.at[:, lanes(peer)], arrived.at[c], o_send.at[peer], o_recv.at[c],
            {"cent": peer},
        )

    def result_from(peer):
        return remote(
            finished.at[:, lanes(peer)], arrived.at[peer], o_send.at[peer], o_recv.at[peer],
            {"cent": peer},
        )

    for j in range(1, m):
        result_to(cent_peer(j)).start()
    out_fine[block_rows(c), :] = own_part[:, lanes(c)]

    for j in range(1, m):
        features_to(cent_peer(j)).wait_send()
    for d in range(n):
        for h in range(HALVES):
            @pl.when(jnp.logical_and(z - d >= 0, z < n - 1))
            def _():
                to_right(z - d, h).wait_send()

            @pl.when(jnp.logical_and(z + d < n, z > 0))
            def _():
                to_left(z + d, h).wait_send()

    for j in range(1, n):
        peer = pts_peer(j)
        new_from(peer).wait_recv()
        new_to(peer).wait_send()
        piece_to(peer).wait_send()
        coarse_mass_to(peer).wait_send()
        mass_to(peer).wait_send()
        sums_to(peer).wait_send()
    for i in range(n):
        out_coarse[i * piece : (i + 1) * piece, :] = coarse_new[i].astype(jnp.float32)

    for j in range(1, m):
        peer = cent_peer(j)
        result_from(peer).wait_recv()
        out_fine[block_rows(peer), :] = arrived[peer].astype(jnp.float32)
    for j in range(1, m):
        result_to(cent_peer(j)).wait_send()


def body(point_codes, shard_scales, coarse_centroids, fine_centroids, block_lists, live_counts):
    n = lax.axis_size("pts")
    m = lax.axis_size("cent")
    points, width = point_codes.shape
    own_blocks = fine_centroids.shape[0] // BLOCK
    quarter = fine_centroids.shape[1]
    slots = block_lists.shape[1]
    every_block = slots == n * own_blocks and own_blocks == m and slots <= NCOARSE
    every_block = every_block and NCOARSE % (16 * m * n) == 0
    if not every_block:
        return general_body(
            point_codes, shard_scales, coarse_centroids, fine_centroids, block_lists, live_counts
        )
    share = NCOARSE // m
    f32, bf16 = jnp.float32, jnp.bfloat16
    dma = pltpu.SemaphoreType.DMA
    vmem = pl.BlockSpec(memory_space=pltpu.VMEM)
    hbm = pl.BlockSpec(memory_space=pl.ANY)
    return pl.pallas_call(
        functools.partial(kernel, n, m),
        out_shape=(
            jax.ShapeDtypeStruct((share, width), f32),
            jax.ShapeDtypeStruct((own_blocks * BLOCK, quarter), f32),
        ),
        in_specs=[hbm, vmem, hbm, hbm, vmem, vmem],
        out_specs=(vmem, vmem),
        scratch_shapes=[
            pltpu.VMEM(point_codes.shape, bf16),
            pltpu.VMEM(coarse_centroids.shape, bf16),
            pltpu.VMEM((n, BLOCK, width), bf16),
            pltpu.VMEM((BLOCK, width), f32),
            pltpu.VMEM((n, BLOCK, width), bf16),
            pltpu.VMEM((n, BLOCK, width), bf16),
            pltpu.VMEM((slots, points), f32),
            pltpu.VMEM((NCOARSE, points), f32),
            pltpu.VMEM((share, width), bf16),
            pltpu.VMEM((share, width), f32),
            pltpu.VMEM((n, share // n, width), bf16),
            pltpu.VMEM((n, share // n, width), bf16),
            pltpu.VMEM((n, 8, 128), f32),
            pltpu.VMEM((n, 8, 128), f32),
            pltpu.VMEM((n, 8, 128), f32),
            pltpu.VMEM((BLOCK, width), bf16),
            pltpu.VMEM((m, BLOCK, quarter), bf16),
            dma((3,)),
        ]
        + [dma((m,))] * 2
        + [dma((n, HALVES))] * 3
        + [dma((n,))] * 10
        + [dma((m,))] * 2,
        compiler_params=pltpu.CompilerParams(
            collective_id=0, has_side_effects=True, vmem_limit_bytes=60 * 1024 * 1024
        ),
    )(
        point_codes,
        shard_scales.reshape(1, -1),
        coarse_centroids,
        fine_centroids,
        block_lists,
        live_counts.reshape(1, 1),
    )


def solution(mesh):
    return jax.shard_map(
        body,
        mesh=mesh,
        in_specs=(
            P(("groups", "pts"), None),
            P(("groups", "pts")),
            P("groups", None),
            P(("groups", "pts"), "cent"),
            P(("groups", "pts"), None),
            P(("groups", "pts")),
        ),
        out_specs=(P(("groups", "cent"), None), P(("groups", "pts"), "cent")),
        check_vma=False,
    )
```
